128 devices in a mesh: rows: 32 (over z, y, core), rep: 4 (over x).
Axes of the slice: x: 4, y: 4, z: 4, core: 2. Of those that a mesh axis runs over, the one named last changes fastest.
Arguments:
- item_table: float32 [524288, 128], P('rows'), may hold values from -6 to 6
- item_ids: int32 [32768, 16], P(('rows', 'rep')), may hold values from 0 to 524287, as said below
- ratings: float32 [32768, 16], P(('rows', 'rep')), may hold values from 0.1 to 10
- counts: int32 [32768], P(('rows', 'rep')), may hold values from 1 to 16
- user_batch: int32 [32768], P(('rows', 'rep')), may hold values from 0 to 32767, as said below
Outputs:
- user_table: float32 [32768, 128], P(('rows', 'rep'))
The draws below stay inside these ranges and needn't reach their ends.
Inputs may be any that keep to these rules, and one draw needn't show every extreme that they name: `item_ids`: each device's 256 x 16 entries name exactly 128 items of every block of 16384 consecutive items, padded entries too. `user_batch`: A permutation of all users; each device's 256 slots hold exactly 2 users of every block of 256 consecutive users.
All inputs are finite; a program needn't handle non-finite values.
Results may differ from the reference program's by a relative error of at most 0.007.
Values sent between devices are 32-bit elements; how exact they have to be, the bound alone decides.
A program may use at most 192 MiB of HBM per device.

```python
import math
import jax
import jax.numpy as jnp
from jax import lax

K = 128
ITEMS_DEV = 16384
L = 16
PER_OWNER = 2
ITERS = 8
U_DEV = 256
USERS = 32768
ITEMS = 524288


def draw_item_table(key, part):
    key = jax.random.fold_in(key, 11)
    base_key, col_key = jax.random.split(key, 2)
    columns = jnp.exp(jax.random.uniform(col_key, (K,), jnp.float32, math.log(0.5), math.log(2.0)))
    rise = 1.0 + 2.0 * jnp.arange(ITEMS, dtype=jnp.float32) / ITEMS
    base = jnp.clip(jax.random.normal(base_key, (ITEMS, K), jnp.float32), -4.0, 4.0)
    return base * columns[None, :] * rise[:, None] / math.sqrt(K)


def draw_item_ids(key, part):
    key = jax.random.fold_in(key, 12)
    shuffle_key, pick_key, skew_key = jax.random.split(key, 3)
    device_count = USERS // U_DEV
    block_count = ITEMS // ITEMS_DEV
    slot_count = U_DEV * L
    owners = jnp.tile(jnp.arange(block_count, dtype=jnp.int32), slot_count // block_count)
    keys = jax.random.split(shuffle_key, device_count)
    shuffled = jax.vmap(lambda one: jax.random.permutation(one, owners))(keys)
    first = jax.random.randint(pick_key, (device_count, slot_count), 0, ITEMS_DEV)
    second = jax.random.randint(skew_key, (device_count, slot_count), 0, ITEMS_DEV)
    inside = jnp.minimum(first, second)
    return (shuffled * ITEMS_DEV + inside).reshape(USERS, L).astype(jnp.int32)


def draw_counts(key, part):
    key = jax.random.fold_in(key, 13)
    drawn = jax.random.randint(key, (USERS,), 1, L + 1)
    drawn = drawn.at[0::U_DEV].set(L)
    drawn = drawn.at[1::U_DEV].set(1)
    return drawn.astype(jnp.int32)


def draw_user_batch(key, part):
    key = jax.random.fold_in(key, 14)
    owner_key, slot_key = jax.random.split(key)
    device_count = USERS // U_DEV
    owner_keys = jax.random.split(owner_key, device_count)
    perms = jax.vmap(lambda one: jax.random.permutation(one, U_DEV))(owner_keys)
    users = perms + (jnp.arange(device_count) * U_DEV)[:, None]
    users = users.reshape(device_count, device_count, PER_OWNER).transpose(1, 0, 2).reshape(device_count, U_DEV)
    slot_keys = jax.random.split(slot_key, device_count)
    mixed = jax.vmap(lambda one, row: jax.random.permutation(one, row))(slot_keys, users)
    return mixed.reshape(USERS).astype(jnp.int32)


def levels(own_key, dims, shards, low, top_value):
    factor_of, own = 1.0, jax.random.fold_in(own_key, 6)
    for dim, shards_of in shards:
        heights = jnp.exp(jax.random.uniform(jax.random.fold_in(own, dim), (shards_of,), jnp.float32, low / len(shards), top_value / len(shards)))
        factor_of = factor_of * jnp.repeat(heights, dims[dim] // shards_of).reshape([-1 if axis == dim else 1 for axis in range(len(dims))])
    return factor_of


def setup_inputs(seed: int = 0) -> dict:
    arg_keys = jax.random.split(jax.random.key(seed), 6)
    item_table = draw_item_table(jax.random.fold_in(arg_keys[5], 71), 0)
    item_ids = draw_item_ids(jax.random.fold_in(arg_keys[5], 71), 0)
    ratings = jnp.clip(jnp.exp(math.log(10.0) - 4.6051702 * jax.random.uniform(arg_keys[2], (USERS, L), jnp.float32) ** levels(arg_keys[2], (USERS, L), ((0, 128),), -0.2, 0.2)), 0.1, 10.0)
    counts = draw_counts(jax.random.fold_in(arg_keys[5], 71), 0)
    user_batch = draw_user_batch(jax.random.fold_in(arg_keys[5], 71), 0)
    return dict(item_table=item_table, item_ids=item_ids, ratings=ratings, counts=counts, user_batch=user_batch)


HIGH = lax.Precision.HIGHEST
REG_WEIGHT = 1.0
GRAM_WEIGHT = 4.0


def solve_users(looked, ratings, counts, scaled):
    length = looked.shape[1]
    live = jnp.arange(length)[None, :] < counts[:, None]
    weight = jnp.where(live, ratings, 0.0)
    pull = jnp.where(live, 1.0 + ratings, 0.0)
    rhs = jnp.einsum("ul,ulk->uk", pull, looked, precision=HIGH)

    def apply(direc):
        proj = jnp.einsum("ulk,uk->ul", looked, direc, precision=HIGH)
        spread = jnp.einsum("ul,ulk->uk", weight * proj, looked, precision=HIGH)
        return jnp.dot(direc, scaled, precision=HIGH) + spread + REG_WEIGHT * direc

    solved = jnp.zeros_like(rhs)
    resid = rhs
    direc = rhs
    norm_now = jnp.sum(resid * resid, axis=1, keepdims=True)
    for step in range(ITERS):
        image = apply(direc)
        alpha = norm_now / jnp.sum(direc * image, axis=1, keepdims=True)
        solved = solved + alpha * direc
        resid = resid - alpha * image
        norm_next = jnp.sum(resid * resid, axis=1, keepdims=True)
        direc = resid + (norm_next / norm_now) * direc
        norm_now = norm_next
    return solved


def reference(item_table, item_ids, ratings, counts, user_batch):
    gram = jnp.dot(item_table.T, item_table, precision=HIGH)
    scaled = gram * (GRAM_WEIGHT * K / ITEMS)
    looked = item_table[item_ids]
    solved = solve_users(looked, ratings, counts, scaled)
    return jnp.zeros((USERS, K), jnp.float32).at[user_batch].set(solved)
```

```python
import functools

import jax
import jax.numpy as jnp
from jax import lax
from jax.experimental import pallas as pl
from jax.experimental.pallas import tpu as pltpu
from jax.sharding import PartitionSpec as P

ITERS = 8
REG_WEIGHT = 1.0
GRAM_WEIGHT = 4.0
HIGH = lax.Precision.HIGHEST
MESH = pl.DeviceIdType.MESH

IDS, ROWS, GRAM_X, PLACE_X, GRAM_SUM, PLACE_ROWS, GRAM_ALL, GRAM_BACK, OUT_X, OUT_ROWS = range(10)


def ring_steps(rows):
    def hops(d):
        dy, dz = (d // 2) % 4, d // 8
        return min(dy, 4 - dy) + min(dz, 4 - dz)

    return sorted(range(1, rows), key=lambda d: (-hops(d), d % 2))


def shifted(me, d):
    c, y, z = me % 2, (me // 2) % 4, me // 8
    dc, dy, dz = d % 2, (d // 2) % 4, d // 8
    return ((z + dz) % 4 * 4 + (y + dy) % 4) * 2 + (c + dc) % 2


def dot(a, b, dims, precision=HIGH):
    return lax.dot_general(a, b, (dims, ((), ())), precision=precision, preferred_element_type=jnp.float32)


def iota(shape, axis):
    return lax.broadcasted_iota(jnp.int32, shape, axis)


def kernel(
    rows, reps, ids_ref, rat_ref, cnt_ref, ub_ref, table_ref, out_ref,
    tv, sendb, recvb, lt, blk, cid, rid, rid_s, pos_v, pos_s,
    gpart, gx, g1, gr, g2, gfull, smat,
    place_a, place_b, place_c, place_d, hot_out, out_a, out_b, out_c, out_d,
    w_s, q_s, x_s, r_s, p_s, ssem, rsem, lsem,
):
    me = lax.axis_index("rows")
    rep = lax.axis_index("rep")
    items = tv.shape[0]
    length, users = ids_ref.shape
    width = tv.shape[1]
    bucket = users * length // rows
    quarter = items // reps
    halves = users // width
    steps = ring_steps(rows)

    def step_of(i):
        d = jnp.int32(steps[0])
        for k in range(1, len(steps)):
            d = jnp.where(i == k, steps[k], d)
        return d

    def table_part(q):
        at = pl.multiple_of(lax.rem(rep + q, reps) * quarter, quarter)
        return pltpu.make_async_copy(table_ref.at[pl.ds(at, quarter)], tv.at[pl.ds(at, quarter)], lsem.at[q])

    for q in range(reps):
        table_part(q).start()

    barrier = pltpu.get_barrier_semaphore()

    def greet(d, c):
        pl.semaphore_signal(barrier, 1, device_id={"rows": shifted(me, d)}, device_id_type=MESH)
        return c

    lax.fori_loop(1, rows, greet, 0)
    for q in range(1, reps):
        pl.semaphore_signal(barrier, 1, device_id={"rep": lax.rem(rep + q, reps)}, device_id_type=MESH)

    ids = jnp.concatenate([ids_ref[:, pl.ds(h * width, width)] for h in range(halves)], axis=0)
    owner = ids // items
    local = ids % items
    local_hi = (local // 128).astype(jnp.float32)
    local_lo = (local % 128).astype(jnp.float32)
    lines = ids.shape[0]
    bucket_id = iota((rows, width), 0)
    hits = [(owner[i:i + 1] == bucket_id).astype(jnp.float32) for i in range(lines)]
    before = (iota((width, width), 0) < iota((width, width), 1)).astype(jnp.float32)
    counter = jnp.concatenate([before, jnp.ones((width, width), jnp.float32)], axis=1).astype(jnp.bfloat16)
    counted = dot(jnp.concatenate(hits, axis=0).astype(jnp.bfloat16), counter, ((1,), (0,)), None)
    seen = jnp.zeros((rows, width), jnp.float32)
    ranks = []
    for i in range(lines):
        part = counted[i * rows:(i + 1) * rows]
        ranks.append(jnp.sum(hits[i] * (part[:, :width] + seen), axis=0, keepdims=True))
        seen = seen + part[:, width:]
    rank = jnp.concatenate(ranks, axis=0).astype(jnp.int32)
    pos_v[...] = jnp.clip(owner * bucket + rank, 0, users * length - 1)
    pltpu.make_async_copy(pos_v, pos_s, lsem.at[reps]).start()
    values = jnp.concatenate([jnp.concatenate([hits[i] * local_hi[i:i + 1], hits[i] * local_lo[i:i + 1]], axis=0) for i in range(lines)], axis=1)
    slots = iota((bucket, width), 0)
    picks = jnp.concatenate([(rank[i:i + 1] == slots).astype(jnp.float32) for i in range(lines)], axis=1)
    compact = dot(values.astype(jnp.bfloat16), picks.astype(jnp.bfloat16), ((1,), (1,)), None)
    compact = jnp.clip((compact[:rows] * 128.0 + compact[rows:]).astype(jnp.int32), 0, items - 1)
    for b in range(rows):
        cid[b] = compact[b:b + 1]

    pl.semaphore_wait(barrier, rows - 1 + reps - 1)

    def to_row(t, src, dst, which):
        return pltpu.make_async_remote_copy(
            src_ref=src, dst_ref=dst, send_sem=ssem.at[which], recv_sem=rsem.at[which],
            device_id={"rows": t}, device_id_type=MESH)

    def to_rep(q, src, dst, which):
        return pltpu.make_async_remote_copy(
            src_ref=src, dst_ref=dst, send_sem=ssem.at[which], recv_sem=rsem.at[which],
            device_id={"rep": q}, device_id_type=MESH)

    def each_row(fn):
        def go(i, c):
            fn(shifted(me, step_of(i)))
            return c

        lax.fori_loop(0, rows - 1, go, 0)

    def each_rep(fn):
        for q in range(1, reps):
            fn(lax.rem(rep + q, reps))

    def drain(sem, ref):
        pltpu.make_async_copy(ref, ref, sem).wait()

    each_row(lambda t: to_row(t, cid.at[t], rid.at[me], IDS).start())
    rid[me] = cid[me]
    for q in range(reps):
        table_part(q).wait()
    drain(rsem.at[IDS], rid.at[pl.ds(0, rows - 1)])
    rid[...] = jnp.clip(rid[...], 0, items - 1)
    ids_copy = pltpu.make_async_copy(rid, rid_s, lsem.at[reps + 1])
    ids_copy.start()
    ids_copy.wait()

    def fetch(t, dst, base):
        for k in range(bucket):
            dst[pl.ds(base + k, 1), :] = tv[pl.ds(rid_s[t, 0, k], 1), :]

    def serve(t):
        base = pl.multiple_of(t * bucket, bucket)
        fetch(t, sendb, base)
        at = pl.multiple_of(me * bucket, bucket)
        to_row(t, sendb.at[pl.ds(base, bucket)], recvb.at[pl.ds(at, bucket)], ROWS).start()

    each_row(serve)
    fetch(me, recvb, pl.multiple_of(me * bucket, bucket))

    share = quarter // 8

    def add_gram(i, total):
        part = tv[pl.ds(pl.multiple_of(rep * quarter + i * share, share), share), :]
        return total + dot(part, part, ((0,), (0,)))

    gpart[...] = lax.fori_loop(0, 8, add_gram, jnp.zeros((width, width), jnp.float32))
    chunk = width // reps

    def chunk_of(q):
        return pl.ds(pl.multiple_of(q * chunk, chunk), chunk)

    each_rep(lambda q: to_rep(q, gpart.at[chunk_of(q)], gx.at[chunk_of(rep)], GRAM_X).start())
    gx[chunk_of(rep), :] = gpart[chunk_of(rep), :]

    ub = ub_ref[...]
    home = ub // users
    home_b = jnp.broadcast_to(home, (users, users))
    home_c = jnp.transpose(home_b)
    earlier = iota((users, users), 0) < iota((users, users), 1)
    twin = jnp.sum(jnp.where(earlier & (home_b == home_c), 1.0, 0.0), axis=0, keepdims=True).astype(jnp.int32)
    per_rep = users // reps
    leave = (home % reps) * per_rep + twin * rows + home // reps
    hot = (iota((users, users), 0) == leave).astype(jnp.float32)
    hot_out[...] = hot
    place = jnp.sum(hot * (ub % users).astype(jnp.float32), axis=1, keepdims=True)
    place_a[...] = jnp.broadcast_to(place, (users, width))

    def block_of(q):
        return pl.ds(pl.multiple_of(q * per_rep, per_rep), per_rep)

    def leave_x(a, b, which):
        each_rep(lambda q: to_rep(q, a.at[block_of(q)], b.at[block_of(rep)], which).start())
        b[block_of(rep), :] = a[block_of(rep), :]
        drain(rsem.at[which], b.at[pl.ds(0, users - per_rep)])

    pieces = users // rows

    def piece_of(t):
        return pl.ds(pl.multiple_of(t * pieces, pieces), pieces)

    def leave_rows(b, c, d, which):
        for t in range(rows):
            for j in range(pieces):
                at = t * pieces + j
                c[at:at + 1, :] = b[j * rows + t:j * rows + t + 1, :]
        each_row(lambda t: to_row(t, c.at[piece_of(t)], d.at[piece_of(me)], which).start())
        d[piece_of(me), :] = c[piece_of(me), :]

    def arrived(d, which):
        drain(rsem.at[which], d.at[pl.ds(0, users - pieces)])

    leave_x(place_a, place_b, PLACE_X)
    leave_rows(place_b, place_c, place_d, PLACE_ROWS)

    drain(rsem.at[GRAM_X], gx.at[pl.ds(0, width - chunk)])
    total = gx[0:chunk, :]
    for q in range(1, reps):
        total = total + gx[q * chunk:(q + 1) * chunk, :]
    for b in range(rows):
        g1[b] = total[b:b + 1]
    each_row(lambda t: to_row(t, g1.at[t], gr.at[me], GRAM_SUM).start())
    gr[me] = g1[me]
    drain(rsem.at[GRAM_SUM], gr.at[pl.ds(0, rows - 1)])
    g2[0] = jnp.sum(gr[...], axis=0)
    each_row(lambda t: to_row(t, g2.at[0], gfull.at[rep, me], GRAM_ALL).start())
    gfull[rep, me] = g2[0]
    drain(rsem.at[GRAM_ALL], gr.at[pl.ds(0, rows - 1)])
    each_rep(lambda q: to_rep(q, gfull.at[rep], gfull.at[rep], GRAM_BACK).start())
    drain(rsem.at[GRAM_BACK], gfull.at[pl.ds(0, reps - 1)])
    scale = GRAM_WEIGHT * width / (items * rows)
    for q in range(reps):
        for b in range(rows):
            smat[q * chunk + b:q * chunk + b + 1, :] = gfull[q, b] * scale
    eye = (iota((width, width), 0) == iota((width, width), 1)).astype(jnp.float32)
    smat[...] = smat[...] + REG_WEIGHT * eye

    arrived(place_d, PLACE_ROWS)
    place = place_d[...].astype(jnp.int32)
    back = jnp.concatenate([(place == iota((users, width), 1) + h * width).astype(jnp.float32) for h in range(halves)], axis=1)

    live = iota((length, users), 0) < cnt_ref[...]
    w_s[...] = jnp.where(live, rat_ref[...], 0.0)
    pulls = jnp.where(live, 1.0 + rat_ref[...], 0.0)
    x_s[...] = jnp.zeros_like(x_s)

    pltpu.make_async_copy(pos_v, pos_s, lsem.at[reps]).wait()
    drain(rsem.at[ROWS], recvb.at[pl.ds(0, (rows - 1) * bucket)])

    def turn(i, c):
        for k in range(width):
            blk[pl.ds(k, 1), :] = recvb[pl.ds(pos_s[i, k], 1), :]
        lt[i] = jnp.transpose(blk[...])
        return c

    lax.fori_loop(0, lines, turn, 0)

    for h in range(halves):
        half = slice(h * width, (h + 1) * width)
        rhs = jnp.zeros((width, width), jnp.float32)
        for l in range(length):
            rhs = rhs + lt[h * length + l] * pulls[l:l + 1, half]
        r_s[:, half] = rhs
        p_s[:, half] = rhs

    def iterate(i, norms):
        q_s[...] = dot(smat[...], p_s[...], ((1,), (0,)))
        out = []
        for h in range(halves):
            half = slice(h * width, (h + 1) * width)
            direc = p_s[:, half]
            image = q_s[:, half]
            for l in range(length):
                rows_l = lt[h * length + l]
                proj = jnp.sum(rows_l * direc, axis=0, keepdims=True)
                image = image + rows_l * (w_s[l:l + 1, half] * proj)
            alpha = norms[h] / jnp.sum(direc * image, axis=0, keepdims=True)
            x_s[:, half] = x_s[:, half] + alpha * direc
            resid = r_s[:, half] - alpha * image
            r_s[:, half] = resid
            norm_next = jnp.sum(resid * resid, axis=0, keepdims=True)
            p_s[:, half] = resid + norm_next / norms[h] * direc
            out.append(norm_next)
        return tuple(out)

    start = []
    for h in range(halves):
        first = r_s[:, h * width:(h + 1) * width]
        start.append(jnp.sum(first * first, axis=0, keepdims=True))
    lax.fori_loop(0, ITERS, iterate, tuple(start))

    out_a[...] = dot(hot_out[...], x_s[...], ((1,), (1,)))
    leave_x(out_a, out_b, OUT_X)
    leave_rows(out_b, out_c, out_d, OUT_ROWS)
    arrived(out_d, OUT_ROWS)
    out_ref[...] = dot(back, out_d[...], ((0,), (0,)))

    drain(ssem.at[IDS], rid.at[pl.ds(0, rows - 1)])
    drain(ssem.at[ROWS], sendb.at[pl.ds(0, (rows - 1) * bucket)])
    drain(ssem.at[GRAM_X], gx.at[pl.ds(0, width - chunk)])
    drain(ssem.at[GRAM_SUM], gr.at[pl.ds(0, rows - 1)])
    drain(ssem.at[GRAM_ALL], gr.at[pl.ds(0, rows - 1)])
    drain(ssem.at[GRAM_BACK], gfull.at[pl.ds(0, reps - 1)])
    drain(ssem.at[PLACE_X], place_b.at[pl.ds(0, users - per_rep)])
    drain(ssem.at[PLACE_ROWS], place_d.at[pl.ds(0, users - pieces)])
    drain(ssem.at[OUT_X], out_b.at[pl.ds(0, users - per_rep)])
    drain(ssem.at[OUT_ROWS], out_d.at[pl.ds(0, users - pieces)])


def body(rows, reps, item_table, item_ids, ratings, counts, user_batch):
    users, length = item_ids.shape
    items, width = item_table.shape
    slots = users * length
    f32, i32 = jnp.float32, jnp.int32
    vmem = pl.BlockSpec(memory_space=pltpu.VMEM)
    square = pltpu.VMEM((width, width), f32)
    wide = pltpu.VMEM((width, users), f32)
    tall = pltpu.VMEM((users, width), f32)
    return pl.pallas_call(
        functools.partial(kernel, rows, reps),
        out_shape=jax.ShapeDtypeStruct((users, width), f32),
        in_specs=[vmem] * 4 + [pl.BlockSpec(memory_space=pl.ANY)],
        out_specs=vmem,
        scratch_shapes=[
            pltpu.VMEM((items, width), f32),
            pltpu.VMEM((slots, width), f32),
            pltpu.VMEM((slots, width), f32),
            pltpu.VMEM((slots // width, width, width), f32),
            square,
            pltpu.VMEM((rows, 1, width), i32),
            pltpu.VMEM((rows, 1, width), i32),
            pltpu.SMEM((rows, 1, width), i32),
            pltpu.VMEM((slots // width, width), i32),
            pltpu.SMEM((slots // width, width), i32),
            square,
            square,
            pltpu.VMEM((rows, 1, width), f32),
            pltpu.VMEM((rows, 1, width), f32),
            pltpu.VMEM((1, 1, width), f32),
            pltpu.VMEM((reps, rows, 1, width), f32),
            square,
            tall, tall, tall, tall,
            pltpu.VMEM((users, users), f32),
            tall, tall, tall, tall,
            pltpu.VMEM((length, users), f32),
            wide, wide, wide, wide,
            pltpu.SemaphoreType.DMA((10,)),
            pltpu.SemaphoreType.DMA((10,)),
            pltpu.SemaphoreType.DMA((reps + 2,)),
        ],
        compiler_params=pltpu.CompilerParams(
            collective_id=0, has_side_effects=True, vmem_limit_bytes=40 << 20
        ),
    )(item_ids.T, ratings.T, counts.reshape(1, users), user_batch.reshape(1, users), item_table)


def solution(mesh):
    in_specs = (
        P("rows", None),
        P(("rows", "rep"), None),
        P(("rows", "rep"), None),
        P(("rows", "rep")),
        P(("rows", "rep")),
    )
    out_specs = P(("rows", "rep"), None)
    step = functools.partial(body, mesh.shape["rows"], mesh.shape["rep"])
    return jax.shard_map(step, mesh=mesh, in_specs=in_specs, out_specs=out_specs, check_vma=False)
```

```python
import functools

import jax
import jax.numpy as jnp
from jax import lax
from jax.experimental import pallas as pl
from jax.experimental.pallas import tpu as pltpu
from jax.sharding import PartitionSpec as P

ITERS = 8
REG_WEIGHT = 1.0
GRAM_WEIGHT = 4.0
HIGH = lax.Precision.HIGHEST
MESH = pl.DeviceIdType.MESH

ROWS, GRAM_X, PLACE_NEAR, GRAM_SUM, PLACE_FAR, GRAM_ALL, GRAM_BACK, OUT_NEAR, OUT_FAR = range(9)


def ring_steps(rows):
    def hops(d):
        dy, dz = (d // 2) % 4, d // 8
        return min(dy, 4 - dy) + min(dz, 4 - dz)

    return sorted(range(1, rows), key=lambda d: (-hops(d), d % 2))


def opposite(d):
    return (4 - d // 8) % 4 * 8 + (4 - d // 2 % 4) % 4 * 2 + d % 2


def shifted(me, d):
    c, y, z = me % 2, (me // 2) % 4, me // 8
    dc, dy, dz = d % 2, (d // 2) % 4, d // 8
    return ((z + dz) % 4 * 4 + (y + dy) % 4) * 2 + (c + dc) % 2


def dot(a, b, dims, precision=HIGH):
    return lax.dot_general(a, b, (dims, ((), ())), precision=precision, preferred_element_type=jnp.float32)


def iota(shape, axis):
    return lax.broadcasted_iota(jnp.int32, shape, axis)


def kernel(
    rows, reps, ids_hbm, rat_hbm, cnt_hbm, ub_hbm, table_ref, out_hbm,
    ids_ref, rat_ref, cnt_ref, ub_ref, out_ref, tv, sendb, recvb, lt, blk_a, blk_b, cid, rid, rid_s, pos_v, pos_s,
    gpart, gx, g1, gr, g2, gfull, smat,
    place_a, place_b, place_c, place_d, inv_v, inv_s, pull_s, out_a, out_b, out_c, out_d,
    w_s, q_s, x_s, r_s, p_s, ssem, rsem, id_ssem, id_rsem, lsem,
):
    me = lax.axis_index("rows")
    rep = lax.axis_index("rep")
    items = tv.shape[0]
    length, users = ids_ref.shape
    width = tv.shape[1]
    bucket = users * length // rows
    quarter = items // reps
    halves = users // width
    steps = ring_steps(rows)

    def step_of(i):
        d = jnp.int32(steps[0])
        for k in range(1, len(steps)):
            d = jnp.where(i == k, steps[k], d)
        return d

    def table_part(q):
        at = pl.multiple_of(lax.rem(rep + q, reps) * quarter, quarter)
        return pltpu.make_async_copy(table_ref.at[pl.ds(at, quarter)], tv.at[pl.ds(at, quarter)], lsem.at[q])

    small = [
        pltpu.make_async_copy(src, dst, lsem.at[reps + 2 + i])
        for i, (src, dst) in enumerate(((ids_hbm, ids_ref), (rat_hbm, rat_ref), (cnt_hbm, cnt_ref), (ub_hbm, ub_ref)))
    ]
    for copy in small:
        copy.start()
    for q in range(reps):
        table_part(q).start()

    barrier = pltpu.get_barrier_semaphore()

    def next_row(i):
        t = me + i
        return jnp.where(t >= rows, t - rows, t)

    def greet(i, c):
        pl.semaphore_signal(barrier, 1, device_id={"rows": next_row(i)}, device_id_type=MESH)
        return c

    lax.fori_loop(1, rows, greet, 0)
    near = 2 * reps
    core = me % 2
    here = core * reps + rep

    def near_peer(i):
        g = lax.rem(here + i, near)
        return g, me - core + g // reps, g % reps

    def greet_near(i, c):
        _, t, q = near_peer(i)
        pl.semaphore_signal(barrier, 1, device_id={"rows": t, "rep": q}, device_id_type=MESH)
        return c

    lax.fori_loop(1, reps, greet_near, 0)
    lax.fori_loop(reps + 1, near, greet_near, 0)

    for copy in small:
        copy.wait()

    ids = jnp.concatenate([ids_ref[:, pl.ds(h * width, width)] for h in range(halves)], axis=0)
    owner = ids // items
    local = ids % items
    local_hi = (local // 128).astype(jnp.float32)
    local_lo = (local % 128).astype(jnp.float32)
    lines = ids.shape[0]
    bucket_id = iota((rows, width), 0)
    hits = [(owner[i:i + 1] == bucket_id).astype(jnp.float32) for i in range(lines)]
    before = (iota((width, width), 0) < iota((width, width), 1)).astype(jnp.float32)
    counter = jnp.concatenate([before, jnp.ones((width, width), jnp.float32)], axis=1).astype(jnp.bfloat16)
    counted = dot(jnp.concatenate(hits, axis=0).astype(jnp.bfloat16), counter, ((1,), (0,)), None)
    seen = jnp.zeros((rows, width), jnp.float32)
    ranks = []
    for i in range(lines):
        part = counted[i * rows:(i + 1) * rows]
        ranks.append(jnp.sum(hits[i] * (part[:, :width] + seen), axis=0, keepdims=True))
        seen = seen + part[:, width:]
    rank = jnp.concatenate(ranks, axis=0).astype(jnp.int32)
    pos_v[...] = owner * bucket + rank
    values = jnp.concatenate([jnp.concatenate([hits[i] * local_hi[i:i + 1], hits[i] * local_lo[i:i + 1]], axis=0) for i in range(lines)], axis=1)
    slots = iota((bucket, width), 0)
    picks = jnp.concatenate([(rank[i:i + 1] == slots).astype(jnp.float32) for i in range(lines)], axis=1)
    compact = dot(values.astype(jnp.bfloat16), picks.astype(jnp.bfloat16), ((1,), (1,)), None)
    compact = jnp.clip((compact[:rows] * 128.0 + compact[rows:]).astype(jnp.int32), 0, items - 1)
    for b in range(rows):
        cid[b] = compact[b:b + 1]

    pl.semaphore_wait(barrier, rows - 1 + near - 2)

    def to_row(t, src, dst, which):
        return pltpu.make_async_remote_copy(
            src_ref=src, dst_ref=dst, send_sem=ssem.at[which], recv_sem=rsem.at[which],
            device_id={"rows": t}, device_id_type=MESH)

    def to_rep(q, src, dst, which):
        return pltpu.make_async_remote_copy(
            src_ref=src, dst_ref=dst, send_sem=ssem.at[which], recv_sem=rsem.at[which],
            device_id={"rep": q}, device_id_type=MESH)

    def each_row(fn):
        def go(i, c):
            fn(next_row(i))
            return c

        lax.fori_loop(1, rows, go, 0)

    def each_rep(fn):
        for q in range(1, reps):
            fn(lax.rem(rep + q, reps))

    def drain(sem, ref):
        pltpu.make_async_copy(ref, ref, sem).wait()

    turned = [lax.rem(me // 8 + dz, 4) * 8 for dz in range(4)]
    beside = [lax.rem(me // 2 + dy, 4) * 2 for dy in range(4)]
    stops = (0, 4, 14, 22, rows - 1)
    for d in steps:
        t = turned[d // 8] + beside[d // 2 % 4] + (core if d % 2 == 0 else 1 - core)
        slot = steps.index(opposite(d))
        which = 0 if slot < stops[1] else 1
        pltpu.make_async_remote_copy(
            src_ref=cid.at[t], dst_ref=rid.at[slot], send_sem=id_ssem.at[0], recv_sem=id_rsem.at[which],
            device_id={"rows": t}, device_id_type=MESH).start()
    rid[rows - 1] = cid[me]

    share = quarter // 8

    def add_gram(i, total):
        part = tv[pl.ds(pl.multiple_of(rep * quarter + i * share, share), share), :]
        return total + dot(part, part, ((0,), (0,)))

    table_part(0).wait()
    gpart[...] = lax.fori_loop(0, 8, add_gram, jnp.zeros((width, width), jnp.float32))
    chunk = width // reps

    def chunk_of(q):
        return pl.ds(pl.multiple_of(q * chunk, chunk), chunk)

    each_rep(lambda q: to_rep(q, gpart.at[chunk_of(q)], gx.at[chunk_of(rep)], GRAM_X).start())
    gx[chunk_of(rep), :] = gpart[chunk_of(rep), :]
    for q in range(1, reps):
        table_part(q).wait()

    def fetch(i, dst, base):
        for k in range(bucket):
            dst[pl.ds(base + k, 1), :] = tv[pl.ds(rid_s[i, 0, k], 1), :]

    def take_ids(part, first, last):
        drain(id_rsem.at[part], rid.at[pl.ds(first, min(last, rows - 1) - first)])
        got = pl.ds(first, last - first)
        rid[got] = jnp.clip(rid[got], 0, items - 1)
        copy = pltpu.make_async_copy(rid.at[got], rid_s.at[got], lsem.at[reps])
        copy.start()
        copy.wait()

    def serve(i, t):
        base = pl.multiple_of(t * bucket, bucket)
        fetch(i, sendb, base)
        after = shifted(me, step_of(i + 1))
        at = pl.multiple_of(me * bucket, bucket)
        to_row(t, sendb.at[pl.ds(base, bucket)], recvb.at[pl.ds(at, bucket)], ROWS).start()
        return after

    take_ids(0, 0, stops[1])
    upcoming = shifted(me, jnp.int32(steps[0]))

    def serve_group(g, t):
        return lax.fori_loop(stops[g], stops[g + 1], serve, t)

    upcoming = serve_group(0, upcoming)
    take_ids(1, stops[1], rows)

    drain(rsem.at[GRAM_X], gx.at[pl.ds(0, width - chunk)])
    total = gx[0:chunk, :]
    for q in range(1, reps):
        total = total + gx[q * chunk:(q + 1) * chunk, :]
    for b in range(rows):
        g1[b] = total[b:b + 1]
    each_row(lambda t: to_row(t, g1.at[t], gr.at[me], GRAM_SUM).start())
    gr[me] = g1[me]

    upcoming = serve_group(1, upcoming)

    ub = ub_ref[...]
    home = ub // users
    home_b = jnp.broadcast_to(home, (users, users))
    home_c = jnp.transpose(home_b)
    earlier = iota((users, users), 0) < iota((users, users), 1)
    twin = jnp.sum(jnp.where(earlier & (home_b == home_c), 1.0, 0.0), axis=0, keepdims=True).astype(jnp.int32)
    group = users // near
    far = rows // 2
    home_row, home_rep = home // reps, home % reps
    leave = ((home_row % 2) * reps + home_rep) * group + twin * far + home_row // 2
    hot = (iota((users, users), 0) == leave).astype(jnp.float32)
    place = jnp.sum(hot * (ub % users).astype(jnp.float32), axis=1, keepdims=True)
    place_a[...] = jnp.broadcast_to(place, (users, width))

    def group_of(g):
        return pl.ds(pl.multiple_of(g * group, group), group)

    def leave_near(a, b, which):
        def go(i, c):
            g, t, q = near_peer(i)
            pltpu.make_async_remote_copy(
                src_ref=a.at[group_of(g)], dst_ref=b.at[group_of(here)], send_sem=ssem.at[which], recv_sem=rsem.at[which],
                device_id={"rows": t, "rep": q}, device_id_type=MESH).start()
            return c

        lax.fori_loop(1, near, go, 0)
        b[group_of(here), :] = a[group_of(here), :]

    pieces = users // far
    spot = me // 2

    def piece_of(t):
        return pl.ds(pl.multiple_of(t * pieces, pieces), pieces)

    def leave_far(b, c, d, before, which):
        drain(rsem.at[before], b.at[pl.ds(0, users - group)])
        for t in range(far):
            for j in range(pieces):
                at = t * pieces + j
                c[at:at + 1, :] = b[j * far + t:j * far + t + 1, :]

        def go(i, k):
            t = lax.rem(spot + i, far)
            to_row(2 * t + core, c.at[piece_of(t)], d.at[piece_of(spot)], which).start()
            return k

        lax.fori_loop(1, far, go, 0)
        d[piece_of(spot), :] = c[piece_of(spot), :]

    def arrived(d, which):
        drain(rsem.at[which], d.at[pl.ds(0, users - pieces)])

    leave_near(place_a, place_b, PLACE_NEAR)

    live = iota((length, users), 0) < cnt_ref[...]
    entry = jnp.concatenate([pos_v[h * length:(h + 1) * length, :] for h in range(halves)], axis=1).astype(jnp.float32)
    lists = jnp.concatenate([jnp.where(live, rat_ref[...], 0.0), jnp.where(live, 1.0 + rat_ref[...], 0.0), entry], axis=0)
    lists = dot(lists, hot, ((1,), (1,)))
    w_s[...] = lists[:length]
    pull_s[...] = lists[length:2 * length]
    entry = jnp.concatenate([lists[2 * length:, h * width:(h + 1) * width] for h in range(halves)], axis=0)
    pos_v[...] = jnp.clip(entry.astype(jnp.int32), 0, users * length - 1)
    pos_copy = pltpu.make_async_copy(pos_v, pos_s, lsem.at[reps + 1])
    pos_copy.start()

    drain(rsem.at[GRAM_SUM], gr.at[pl.ds(0, rows - 1)])
    g2[0] = jnp.sum(gr[...], axis=0)
    each_row(lambda t: to_row(t, g2.at[0], gfull.at[rep, me], GRAM_ALL).start())
    gfull[rep, me] = g2[0]

    upcoming = serve_group(2, upcoming)
    drain(rsem.at[GRAM_ALL], gr.at[pl.ds(0, rows - 1)])
    each_rep(lambda q: to_rep(q, gfull.at[rep], gfull.at[rep], GRAM_BACK).start())
    leave_far(place_b, place_c, place_d, PLACE_NEAR, PLACE_FAR)

    upcoming = serve_group(3, upcoming)
    fetch(rows - 1, recvb, pl.multiple_of(me * bucket, bucket))
    drain(rsem.at[GRAM_BACK], gfull.at[pl.ds(0, reps - 1)])
    scale = GRAM_WEIGHT * width / (items * rows)
    for q in range(reps):
        for b in range(rows):
            smat[q * chunk + b:q * chunk + b + 1, :] = gfull[q, b] * scale
    eye = (iota((width, width), 0) == iota((width, width), 1)).astype(jnp.float32)
    smat[...] = smat[...] + REG_WEIGHT * eye

    arrived(place_d, PLACE_FAR)
    place = place_d[...].astype(jnp.int32)
    came = iota((users, width), 0).astype(jnp.float32)
    for h in range(halves):
        here_is = jnp.where(place == iota((users, width), 1) + h * width, came, 0.0)
        inv_v[h:h + 1, :] = jnp.clip(jnp.sum(here_is, axis=0, keepdims=True).astype(jnp.int32), 0, users - 1)
    inv_copy = pltpu.make_async_copy(inv_v, inv_s, lsem.at[0])
    inv_copy.start()
    x_s[...] = jnp.zeros_like(x_s)
    inv_copy.wait()
    pos_copy.wait()
    drain(rsem.at[ROWS], recvb.at[pl.ds(0, (rows - 1) * bucket)])

    def gather(i, dst):
        for k in range(width):
            dst[pl.ds(k, 1), :] = recvb[pl.ds(pos_s[i, k], 1), :]

    def turn(i, c):
        gather(2 * i + 1, blk_b)
        lt[2 * i] = jnp.transpose(blk_a[...])
        gather(jnp.minimum(2 * i + 2, lines - 1), blk_a)
        lt[2 * i + 1] = jnp.transpose(blk_b[...])
        return c

    gather(0, blk_a)
    lax.fori_loop(0, lines // 2, turn, 0)

    for h in range(halves):
        half = slice(h * width, (h + 1) * width)
        rhs = jnp.zeros((width, width), jnp.float32)
        for l in range(length):
            rhs = rhs + lt[h * length + l] * pull_s[l:l + 1, half]
        r_s[:, half] = rhs
        p_s[:, half] = rhs

    def iterate(i, norms):
        q_s[...] = dot(smat[...], p_s[...], ((1,), (0,)))
        out = []
        for h in range(halves):
            half = slice(h * width, (h + 1) * width)
            direc = p_s[:, half]
            image = jnp.zeros((width, width), jnp.float32)
            for l in range(length):
                rows_l = lt[h * length + l]
                proj = jnp.sum(rows_l * direc, axis=0, keepdims=True)
                image = image + rows_l * (w_s[l:l + 1, half] * proj)
            image = image + q_s[:, half]
            alpha = norms[h] / jnp.sum(direc * image, axis=0, keepdims=True)
            x_s[:, half] = x_s[:, half] + alpha * direc
            resid = r_s[:, half] - alpha * image
            r_s[:, half] = resid
            norm_next = jnp.sum(resid * resid, axis=0, keepdims=True)
            p_s[:, half] = resid + norm_next / norms[h] * direc
            out.append(norm_next)
        return tuple(out)

    start = []
    for h in range(halves):
        first = r_s[:, h * width:(h + 1) * width]
        start.append(jnp.sum(first * first, axis=0, keepdims=True))
    lax.fori_loop(0, ITERS, iterate, tuple(start))

    for h in range(halves):
        out_a[h * width:(h + 1) * width, :] = jnp.transpose(x_s[:, h * width:(h + 1) * width])
    leave_near(out_a, out_b, OUT_NEAR)
    leave_far(out_b, out_c, out_d, OUT_NEAR, OUT_FAR)
    arrived(out_d, OUT_FAR)
    for h in range(halves):
        for k in range(width):
            at = h * width + k
            out_ref[at:at + 1, :] = out_d[pl.ds(inv_s[h, k], 1), :]
    result = pltpu.make_async_copy(out_ref, out_hbm, lsem.at[0])
    result.start()

    drain(id_ssem.at[0], cid.at[pl.ds(0, rows - 1)])
    drain(ssem.at[ROWS], sendb.at[pl.ds(0, (rows - 1) * bucket)])
    drain(ssem.at[GRAM_X], gx.at[pl.ds(0, width - chunk)])
    drain(ssem.at[GRAM_SUM], gr.at[pl.ds(0, rows - 1)])
    drain(ssem.at[GRAM_ALL], gr.at[pl.ds(0, rows - 1)])
    drain(ssem.at[GRAM_BACK], gfull.at[pl.ds(0, reps - 1)])
    drain(ssem.at[PLACE_NEAR], place_b.at[pl.ds(0, users - group)])
    drain(ssem.at[PLACE_FAR], place_d.at[pl.ds(0, users - pieces)])
    drain(ssem.at[OUT_NEAR], out_b.at[pl.ds(0, users - group)])
    drain(ssem.at[OUT_FAR], out_d.at[pl.ds(0, users - pieces)])
    result.wait()


def body(rows, reps, item_table, item_ids, ratings, counts, user_batch):
    users, length = item_ids.shape
    items, width = item_table.shape
    slots = users * length
    f32, i32 = jnp.float32, jnp.int32
    hbm = pl.BlockSpec(memory_space=pltpu.HBM)
    square = pltpu.VMEM((width, width), f32)
    wide = pltpu.VMEM((width, users), f32)
    tall = pltpu.VMEM((users, width), f32)
    return pl.pallas_call(
        functools.partial(kernel, rows, reps),
        out_shape=jax.ShapeDtypeStruct((users, width), f32),
        in_specs=[hbm] * 5,
        out_specs=hbm,
        scratch_shapes=[
            pltpu.VMEM((length, users), i32),
            pltpu.VMEM((length, users), f32),
            pltpu.VMEM((1, users), i32),
            pltpu.VMEM((1, users), i32),
            tall,
            pltpu.VMEM((items, width), f32),
            pltpu.VMEM((slots, width), f32),
            pltpu.VMEM((slots, width), f32),
            pltpu.VMEM((slots // width, width, width), f32),
            square, square,
            pltpu.VMEM((rows, 1, width), i32),
            pltpu.VMEM((rows, 1, width), i32),
            pltpu.SMEM((rows, 1, width), i32),
            pltpu.VMEM((slots // width, width), i32),
            pltpu.SMEM((slots // width, width), i32),
            square,
            square,
            pltpu.VMEM((rows, 1, width), f32),
            pltpu.VMEM((rows, 1, width), f32),
            pltpu.VMEM((1, 1, width), f32),
            pltpu.VMEM((reps, rows, 1, width), f32),
            square,
            tall, tall, tall, tall,
            pltpu.VMEM((users // width, width), i32),
            pltpu.SMEM((users // width, width), i32),
            pltpu.VMEM((length, users), f32),
            tall, tall, tall, tall,
            pltpu.VMEM((length, users), f32),
            wide, wide, wide, wide,
            pltpu.SemaphoreType.DMA((9,)),
            pltpu.SemaphoreType.DMA((9,)),
            pltpu.SemaphoreType.DMA((1,)),
            pltpu.SemaphoreType.DMA((2,)),
            pltpu.SemaphoreType.DMA((reps + 6,)),
        ],
        compiler_params=pltpu.CompilerParams(
            collective_id=0, has_side_effects=True, vmem_limit_bytes=63 << 20
        ),
    )(item_ids.T, ratings.T, counts.reshape(1, users), user_batch.reshape(1, users), item_table)


def solution(mesh):
    in_specs = (
        P("rows", None),
        P(("rows", "rep"), None),
        P(("rows", "rep"), None),
        P(("rows", "rep")),
        P(("rows", "rep")),
    )
    out_specs = P(("rows", "rep"), None)
    step = functools.partial(body, mesh.shape["rows"], mesh.shape["rep"])
    return jax.shard_map(step, mesh=mesh, in_specs=in_specs, out_specs=out_specs, check_vma=False)
```

```python
import functools

import jax
import jax.numpy as jnp
from jax import lax
from jax.experimental import pallas as pl
from jax.experimental.pallas import tpu as pltpu
from jax.sharding import PartitionSpec as P

ITERS = 8
REG_WEIGHT = 1.0
GRAM_WEIGHT = 4.0
HIGH = lax.Precision.HIGHEST
MESH = pl.DeviceIdType.MESH

ROWS, GRAM_X, PLACE_NEAR, GRAM_SUM, PLACE_FAR, GRAM_ALL, GRAM_BACK, OUT = range(8)


def ring_steps(rows):
    def hops(d):
        dy, dz = (d // 2) % 4, d // 8
        return min(dy, 4 - dy) + min(dz, 4 - dz)

    return sorted(range(1, rows), key=lambda d: (-hops(d), d % 2))


def opposite(d):
    return (4 - d // 8) % 4 * 8 + (4 - d // 2 % 4) % 4 * 2 + d % 2


def shifted(me, d):
    c, y, z = me % 2, (me // 2) % 4, me // 8
    dc, dy, dz = d % 2, (d // 2) % 4, d // 8
    return ((z + dz) % 4 * 4 + (y + dy) % 4) * 2 + (c + dc) % 2


def dot(a, b, dims, precision=HIGH):
    return lax.dot_general(a, b, (dims, ((), ())), precision=precision, preferred_element_type=jnp.float32)


def iota(shape, axis):
    return lax.broadcasted_iota(jnp.int32, shape, axis)


def kernel(
    rows, reps, ids_hbm, rat_hbm, cnt_hbm, ub_hbm, table_ref, out_hbm,
    ids_ref, rat_ref, cnt_ref, ub_ref, out_ref, tv, sendb, recvb, lt, blk_a, blk_b, cid, rid, rid_s, pos_v, pos_s,
    gpart, gx, g1, gr, g2, gfull, smat,
    place_a, place_b, place_c, place_d, inv_v, inv_s, pull_s, out_a, out_b, out_d,
    w_s, q_s, x_s, r_s, p_s, ssem, rsem, id_ssem, id_rsem, lsem,
):
    me = lax.axis_index("rows")
    rep = lax.axis_index("rep")
    items = tv.shape[0]
    length, users = ids_ref.shape
    width = tv.shape[1]
    bucket = users * length // rows
    quarter = items // reps
    halves = users // width
    steps = ring_steps(rows)

    def step_of(i):
        d = jnp.int32(steps[0])
        for k in range(1, len(steps)):
            d = jnp.where(i == k, steps[k], d)
        return d

    def table_part(q):
        at = pl.multiple_of(lax.rem(rep + q, reps) * quarter, quarter)
        return pltpu.make_async_copy(table_ref.at[pl.ds(at, quarter)], tv.at[pl.ds(at, quarter)], lsem.at[q])

    small = [
        pltpu.make_async_copy(src, dst, lsem.at[reps + 2 + i])
        for i, (src, dst) in enumerate(((ids_hbm, ids_ref), (rat_hbm, rat_ref), (cnt_hbm, cnt_ref), (ub_hbm, ub_ref)))
    ]
    for copy in small:
        copy.start()
    for q in range(reps):
        table_part(q).start()

    barrier = pltpu.get_barrier_semaphore()

    def next_row(i):
        t = me + i
        return jnp.where(t >= rows, t - rows, t)

    def greet(i, c):
        pl.semaphore_signal(barrier, 1, device_id={"rows": next_row(i)}, device_id_type=MESH)
        return c

    lax.fori_loop(1, rows, greet, 0)
    near = 2 * reps
    core = me % 2
    here = core * reps + rep

    def near_peer(i):
        g = lax.rem(here + i, near)
        return g, me - core + g // reps, g % reps

    def greet_near(i, c):
        _, t, q = near_peer(i)
        pl.semaphore_signal(barrier, 1, device_id={"rows": t, "rep": q}, device_id_type=MESH)
        return c

    lax.fori_loop(1, reps, greet_near, 0)
    lax.fori_loop(reps + 1, near, greet_near, 0)

    for copy in small:
        copy.wait()

    ids = jnp.concatenate([ids_ref[:, pl.ds(h * width, width)] for h in range(halves)], axis=0)
    owner = ids // items
    local = ids % items
    local_hi = (local // 128).astype(jnp.float32)
    local_lo = (local % 128).astype(jnp.float32)
    lines = ids.shape[0]
    bucket_id = iota((rows, width), 0)
    hits = [(owner[i:i + 1] == bucket_id).astype(jnp.float32) for i in range(lines)]
    before = (iota((width, width), 0) < iota((width, width), 1)).astype(jnp.float32)
    counter = jnp.concatenate([before, jnp.ones((width, width), jnp.float32)], axis=1).astype(jnp.bfloat16)
    counted = dot(jnp.concatenate(hits, axis=0).astype(jnp.bfloat16), counter, ((1,), (0,)), None)
    seen = jnp.zeros((rows, width), jnp.float32)
    ranks = []
    for i in range(lines):
        part = counted[i * rows:(i + 1) * rows]
        ranks.append(jnp.sum(hits[i] * (part[:, :width] + seen), axis=0, keepdims=True))
        seen = seen + part[:, width:]
    rank = jnp.concatenate(ranks, axis=0).astype(jnp.int32)
    pos_v[...] = owner * bucket + rank
    values = jnp.concatenate([jnp.concatenate([hits[i] * local_hi[i:i + 1], hits[i] * local_lo[i:i + 1]], axis=0) for i in range(lines)], axis=1)
    slots = iota((bucket, width), 0)
    picks = jnp.concatenate([(rank[i:i + 1] == slots).astype(jnp.float32) for i in range(lines)], axis=1)
    compact = dot(values.astype(jnp.bfloat16), picks.astype(jnp.bfloat16), ((1,), (1,)), None)
    compact = jnp.clip((compact[:rows] * 128.0 + compact[rows:]).astype(jnp.int32), 0, items - 1)
    for b in range(rows):
        cid[b] = compact[b:b + 1]

    pl.semaphore_wait(barrier, rows - 1 + near - 2)

    def to_row(t, src, dst, which):
        return pltpu.make_async_remote_copy(
            src_ref=src, dst_ref=dst, send_sem=ssem.at[which], recv_sem=rsem.at[which],
            device_id={"rows": t}, device_id_type=MESH)

    def to_rep(q, src, dst, which):
        return pltpu.make_async_remote_copy(
            src_ref=src, dst_ref=dst, send_sem=ssem.at[which], recv_sem=rsem.at[which],
            device_id={"rep": q}, device_id_type=MESH)

    def each_row(fn):
        def go(i, c):
            fn(next_row(i))
            return c

        lax.fori_loop(1, rows, go, 0)

    def each_rep(fn):
        for q in range(1, reps):
            fn(lax.rem(rep + q, reps))

    def drain(sem, ref):
        pltpu.make_async_copy(ref, ref, sem).wait()

    turned = [lax.rem(me // 8 + dz, 4) * 8 for dz in range(4)]
    beside = [lax.rem(me // 2 + dy, 4) * 2 for dy in range(4)]
    stops = (0, 4, 14, 22, rows - 1)
    for d in steps:
        t = turned[d // 8] + beside[d // 2 % 4] + (core if d % 2 == 0 else 1 - core)
        slot = steps.index(opposite(d))
        which = 0 if slot < stops[1] else 1
        pltpu.make_async_remote_copy(
            src_ref=cid.at[t], dst_ref=rid.at[slot], send_sem=id_ssem.at[0], recv_sem=id_rsem.at[which],
            device_id={"rows": t}, device_id_type=MESH).start()
    rid[rows - 1] = cid[me]

    share = quarter // 8

    def add_gram(i, total):
        part = tv[pl.ds(pl.multiple_of(rep * quarter + i * share, share), share), :]
        return total + dot(part, part, ((0,), (0,)))

    table_part(0).wait()
    gpart[...] = lax.fori_loop(0, 8, add_gram, jnp.zeros((width, width), jnp.float32))
    chunk = width // reps

    def chunk_of(q):
        return pl.ds(pl.multiple_of(q * chunk, chunk), chunk)

    each_rep(lambda q: to_rep(q, gpart.at[chunk_of(q)], gx.at[chunk_of(rep)], GRAM_X).start())
    gx[chunk_of(rep), :] = gpart[chunk_of(rep), :]
    for q in range(1, reps):
        table_part(q).wait()

    def fetch(i, dst, base):
        for k in range(bucket):
            dst[pl.ds(base + k, 1), :] = tv[pl.ds(rid_s[i, 0, k], 1), :]

    def take_ids(part, first, last):
        drain(id_rsem.at[part], rid.at[pl.ds(first, min(last, rows - 1) - first)])
        got = pl.ds(first, last - first)
        rid[got] = jnp.clip(rid[got], 0, items - 1)
        copy = pltpu.make_async_copy(rid.at[got], rid_s.at[got], lsem.at[reps])
        copy.start()
        copy.wait()

    def serve(i, t):
        base = pl.multiple_of(t * bucket, bucket)
        fetch(i, sendb, base)
        after = shifted(me, step_of(i + 1))
        at = pl.multiple_of(me * bucket, bucket)
        to_row(t, sendb.at[pl.ds(base, bucket)], recvb.at[pl.ds(at, bucket)], ROWS).start()
        return after

    take_ids(0, 0, stops[1])
    upcoming = shifted(me, jnp.int32(steps[0]))

    def serve_group(g, t):
        return lax.fori_loop(stops[g], stops[g + 1], serve, t)

    upcoming = serve_group(0, upcoming)
    take_ids(1, stops[1], rows)

    drain(rsem.at[GRAM_X], gx.at[pl.ds(0, width - chunk)])
    total = gx[0:chunk, :]
    for q in range(1, reps):
        total = total + gx[q * chunk:(q + 1) * chunk, :]
    for b in range(rows):
        g1[b] = total[b:b + 1]
    each_row(lambda t: to_row(t, g1.at[t], gr.at[me], GRAM_SUM).start())
    gr[me] = g1[me]

    upcoming = serve_group(1, upcoming)

    ub = ub_ref[...]
    home = ub // users
    home_b = jnp.broadcast_to(home, (users, users))
    home_c = jnp.transpose(home_b)
    earlier = iota((users, users), 0) < iota((users, users), 1)
    twin = jnp.sum(jnp.where(earlier & (home_b == home_c), 1.0, 0.0), axis=0, keepdims=True).astype(jnp.int32)
    group = users // near
    far = rows // 2
    home_row, home_rep = home // reps, home % reps
    leave = ((home_row % 2) * reps + home_rep) * group + twin * far + home_row // 2
    hot = (iota((users, users), 0) == home * 2 + twin).astype(jnp.float32)
    hot_near = (iota((users, users), 0) == leave).astype(jnp.float32)
    place = jnp.sum(hot_near * (ub % users).astype(jnp.float32), axis=1, keepdims=True)
    place_a[...] = jnp.broadcast_to(place, (users, width))

    def group_of(g):
        return pl.ds(pl.multiple_of(g * group, group), group)

    def leave_near(a, b, which):
        def go(i, c):
            g, t, q = near_peer(i)
            pltpu.make_async_remote_copy(
                src_ref=a.at[group_of(g)], dst_ref=b.at[group_of(here)], send_sem=ssem.at[which], recv_sem=rsem.at[which],
                device_id={"rows": t, "rep": q}, device_id_type=MESH).start()
            return c

        lax.fori_loop(1, near, go, 0)
        b[group_of(here), :] = a[group_of(here), :]

    pieces = users // far
    spot = me // 2

    def piece_of(t):
        return pl.ds(pl.multiple_of(t * pieces, pieces), pieces)

    def leave_far(b, c, d, before, which):
        drain(rsem.at[before], b.at[pl.ds(0, users - group)])
        for t in range(far):
            for j in range(pieces):
                at = t * pieces + j
                c[at:at + 1, :] = b[j * far + t:j * far + t + 1, :]

        def go(i, k):
            t = lax.rem(spot + i, far)
            to_row(2 * t + core, c.at[piece_of(t)], d.at[piece_of(spot)], which).start()
            return k

        lax.fori_loop(1, far, go, 0)
        d[piece_of(spot), :] = c[piece_of(spot), :]

    def arrived(d, which):
        drain(rsem.at[which], d.at[pl.ds(0, users - pieces)])

    leave_near(place_a, place_b, PLACE_NEAR)

    live = iota((length, users), 0) < cnt_ref[...]
    entry = jnp.concatenate([pos_v[h * length:(h + 1) * length, :] for h in range(halves)], axis=1).astype(jnp.float32)
    lists = jnp.concatenate([jnp.where(live, rat_ref[...], 0.0), jnp.where(live, 1.0 + rat_ref[...], 0.0), entry], axis=0)
    lists = dot(lists, hot, ((1,), (1,)))
    w_s[...] = lists[:length]
    pull_s[...] = lists[length:2 * length]
    entry = jnp.concatenate([lists[2 * length:, h * width:(h + 1) * width] for h in range(halves)], axis=0)
    pos_v[...] = jnp.clip(entry.astype(jnp.int32), 0, users * length - 1)
    pos_copy = pltpu.make_async_copy(pos_v, pos_s, lsem.at[reps + 1])
    pos_copy.start()

    drain(rsem.at[GRAM_SUM], gr.at[pl.ds(0, rows - 1)])
    g2[0] = jnp.sum(gr[...], axis=0)
    each_row(lambda t: to_row(t, g2.at[0], gfull.at[rep, me], GRAM_ALL).start())
    gfull[rep, me] = g2[0]

    upcoming = serve_group(2, upcoming)
    drain(rsem.at[GRAM_ALL], gr.at[pl.ds(0, rows - 1)])
    each_rep(lambda q: to_rep(q, gfull.at[rep], gfull.at[rep], GRAM_BACK).start())
    leave_far(place_b, place_c, place_d, PLACE_NEAR, PLACE_FAR)

    upcoming = serve_group(3, upcoming)
    fetch(rows - 1, recvb, pl.multiple_of(me * bucket, bucket))
    drain(rsem.at[GRAM_BACK], gfull.at[pl.ds(0, reps - 1)])
    scale = GRAM_WEIGHT * width / (items * rows)
    for q in range(reps):
        for b in range(rows):
            smat[q * chunk + b:q * chunk + b + 1, :] = gfull[q, b] * scale
    eye = (iota((width, width), 0) == iota((width, width), 1)).astype(jnp.float32)
    smat[...] = smat[...] + REG_WEIGHT * eye

    arrived(place_d, PLACE_FAR)
    place = place_d[...].astype(jnp.int32)
    came = iota((users, width), 0).astype(jnp.float32)
    for h in range(halves):
        here_is = jnp.where(place == iota((users, width), 1) + h * width, came, 0.0)
        inv_v[h:h + 1, :] = jnp.clip(jnp.sum(here_is, axis=0, keepdims=True).astype(jnp.int32), 0, users - 1)
    inv_copy = pltpu.make_async_copy(inv_v, inv_s, lsem.at[0])
    inv_copy.start()
    x_s[...] = jnp.zeros_like(x_s)
    inv_copy.wait()
    pos_copy.wait()
    drain(rsem.at[ROWS], recvb.at[pl.ds(0, (rows - 1) * bucket)])

    def gather(i, dst):
        for k in range(width):
            dst[pl.ds(k, 1), :] = recvb[pl.ds(pos_s[i, k], 1), :]

    def turn(i, c):
        gather(2 * i + 1, blk_b)
        lt[2 * i] = jnp.transpose(blk_a[...])
        gather(jnp.minimum(2 * i + 2, lines - 1), blk_a)
        lt[2 * i + 1] = jnp.transpose(blk_b[...])
        return c

    gather(0, blk_a)
    lax.fori_loop(0, lines // 2, turn, 0)

    for h in range(halves):
        half = slice(h * width, (h + 1) * width)
        rhs = jnp.zeros((width, width), jnp.float32)
        for l in range(length):
            rhs = rhs + lt[h * length + l] * pull_s[l:l + 1, half]
        r_s[:, half] = rhs
        p_s[:, half] = rhs

    def iterate(i, norms):
        q_s[...] = dot(smat[...], p_s[...], ((1,), (0,)))
        out = []
        for h in range(halves):
            half = slice(h * width, (h + 1) * width)
            direc = p_s[:, half]
            image = jnp.zeros((width, width), jnp.float32)
            for l in range(length):
                rows_l = lt[h * length + l]
                proj = jnp.sum(rows_l * direc, axis=0, keepdims=True)
                image = image + rows_l * (w_s[l:l + 1, half] * proj)
            image = image + q_s[:, half]
            alpha = norms[h] / jnp.sum(direc * image, axis=0, keepdims=True)
            x_s[:, half] = x_s[:, half] + alpha * direc
            resid = r_s[:, half] - alpha * image
            r_s[:, half] = resid
            norm_next = jnp.sum(resid * resid, axis=0, keepdims=True)
            p_s[:, half] = resid + norm_next / norms[h] * direc
            out.append(norm_next)
        return tuple(out)

    start = []
    for h in range(halves):
        first = r_s[:, h * width:(h + 1) * width]
        start.append(jnp.sum(first * first, axis=0, keepdims=True))
    lax.fori_loop(0, ITERS, iterate, tuple(start))

    for h in range(halves):
        out_a[h * width:(h + 1) * width, :] = jnp.transpose(x_s[:, h * width:(h + 1) * width])
    devices = rows * reps
    mine = me * reps + rep

    def pair_of(t):
        return pl.ds(2 * t, 2)

    def leave_home(i, c):
        t = mine + i
        t = jnp.where(t >= devices, t - devices, t)
        for j in range(2):
            out_b[2 * t + j] = out_a[pl.ds(2 * t + j, 1), :]
        pltpu.make_async_remote_copy(
            src_ref=out_b.at[pair_of(t)], dst_ref=out_d.at[pair_of(mine)], send_sem=ssem.at[OUT], recv_sem=rsem.at[OUT],
            device_id={"rows": t // reps, "rep": t % reps}, device_id_type=MESH).start()
        return c

    lax.fori_loop(1, devices, leave_home, 0)
    for j in range(2):
        out_d[2 * mine + j] = out_a[pl.ds(2 * mine + j, 1), :]
    drain(rsem.at[OUT], out_d.at[pl.ds(0, users - 2)])
    for h in range(halves):
        for k in range(width):
            at = h * width + k
            out_ref[at:at + 1, :] = out_d[inv_s[h, k]]
    result = pltpu.make_async_copy(out_ref, out_hbm, lsem.at[0])
    result.start()

    drain(id_ssem.at[0], cid.at[pl.ds(0, rows - 1)])
    drain(ssem.at[ROWS], sendb.at[pl.ds(0, (rows - 1) * bucket)])
    drain(ssem.at[GRAM_X], gx.at[pl.ds(0, width - chunk)])
    drain(ssem.at[GRAM_SUM], gr.at[pl.ds(0, rows - 1)])
    drain(ssem.at[GRAM_ALL], gr.at[pl.ds(0, rows - 1)])
    drain(ssem.at[GRAM_BACK], gfull.at[pl.ds(0, reps - 1)])
    drain(ssem.at[PLACE_NEAR], place_b.at[pl.ds(0, users - group)])
    drain(ssem.at[PLACE_FAR], place_d.at[pl.ds(0, users - pieces)])
    drain(ssem.at[OUT], out_b.at[pl.ds(0, users - 2)])
    result.wait()


def body(rows, reps, item_table, item_ids, ratings, counts, user_batch):
    users, length = item_ids.shape
    items, width = item_table.shape
    slots = users * length
    f32, i32 = jnp.float32, jnp.int32
    hbm = pl.BlockSpec(memory_space=pltpu.HBM)
    square = pltpu.VMEM((width, width), f32)
    wide = pltpu.VMEM((width, users), f32)
    single = pltpu.VMEM((users, 1, width), f32)
    tall = pltpu.VMEM((users, width), f32)
    return pl.pallas_call(
        functools.partial(kernel, rows, reps),
        out_shape=jax.ShapeDtypeStruct((users, width), f32),
        in_specs=[hbm] * 5,
        out_specs=hbm,
        scratch_shapes=[
            pltpu.VMEM((length, users), i32),
            pltpu.VMEM((length, users), f32),
            pltpu.VMEM((1, users), i32),
            pltpu.VMEM((1, users), i32),
            tall,
            pltpu.VMEM((items, width), f32),
            pltpu.VMEM((slots, width), f32),
            pltpu.VMEM((slots, width), f32),
            pltpu.VMEM((slots // width, width, width), f32),
            square, square,
            pltpu.VMEM((rows, 1, width), i32),
            pltpu.VMEM((rows, 1, width), i32),
            pltpu.SMEM((rows, 1, width), i32),
            pltpu.VMEM((slots // width, width), i32),
            pltpu.SMEM((slots // width, width), i32),
            square,
            square,
            pltpu.VMEM((rows, 1, width), f32),
            pltpu.VMEM((rows, 1, width), f32),
            pltpu.VMEM((1, 1, width), f32),
            pltpu.VMEM((reps, rows, 1, width), f32),
            square,
            tall, tall, tall, tall,
            pltpu.VMEM((users // width, width), i32),
            pltpu.SMEM((users // width, width), i32),
            pltpu.VMEM((length, users), f32),
            tall, single, single,
            pltpu.VMEM((length, users), f32),
            wide, wide, wide, wide,
            pltpu.SemaphoreType.DMA((8,)),
            pltpu.SemaphoreType.DMA((8,)),
            pltpu.SemaphoreType.DMA((1,)),
            pltpu.SemaphoreType.DMA((2,)),
            pltpu.SemaphoreType.DMA((reps + 6,)),
        ],
        compiler_params=pltpu.CompilerParams(
            collective_id=0, has_side_effects=True, vmem_limit_bytes=63 << 20
        ),
    )(item_ids.T, ratings.T, counts.reshape(1, users), user_batch.reshape(1, users), item_table)


def solution(mesh):
    in_specs = (
        P("rows", None),
        P(("rows", "rep"), None),
        P(("rows", "rep"), None),
        P(("rows", "rep")),
        P(("rows", "rep")),
    )
    out_specs = P(("rows", "rep"), None)
    step = functools.partial(body, mesh.shape["rows"], mesh.shape["rep"])
    return jax.shard_map(step, mesh=mesh, in_specs=in_specs, out_specs=out_specs, check_vma=False)
```

```python
import functools

import jax
import jax.numpy as jnp
from jax import lax
from jax.experimental import pallas as pl
from jax.experimental.pallas import tpu as pltpu
from jax.sharding import PartitionSpec as P

ITERS = 8
REG_WEIGHT = 1.0
GRAM_WEIGHT = 4.0
HIGH = lax.Precision.HIGHEST
MESH = pl.DeviceIdType.MESH

EARLY, LATE, GRAM_X, PLACE_NEAR, GRAM_SUM, PLACE_FAR, GRAM_ALL, GRAM_BACK, OUT = range(9)


def ring_steps(rows):
    def hops(d):
        dy, dz = (d // 2) % 4, d // 8
        return min(dy, 4 - dy) + min(dz, 4 - dz) or 1.5

    return sorted(range(1, rows), key=lambda d: (-hops(d), d % 2))


def opposite(d):
    return (4 - d // 8) % 4 * 8 + (4 - d // 2 % 4) % 4 * 2 + d % 2


def shifted(me, d):
    c, y, z = me % 2, (me // 2) % 4, me // 8
    dc, dy, dz = d % 2, (d // 2) % 4, d // 8
    return ((z + dz) % 4 * 4 + (y + dy) % 4) * 2 + (c + dc) % 2


def dot(a, b, dims, precision=HIGH):
    return lax.dot_general(a, b, (dims, ((), ())), precision=precision, preferred_element_type=jnp.float32)


def halve(a):
    high = a.astype(jnp.bfloat16)
    return high, (a - high.astype(jnp.float32)).astype(jnp.bfloat16)


def iota(shape, axis):
    return lax.broadcasted_iota(jnp.int32, shape, axis)


def kernel(
    rows, reps, ids_hbm, rat_hbm, cnt_hbm, ub_hbm, table_ref, out_hbm,
    ids_ref, rat_ref, cnt_ref, ub_ref, out_ref, tv, sendb, earlyb, lateb, late_v, late_hot, late_turned, lt, blk_a, blk_b, cid, rid, rid_s, pos_v, pos_s,
    gpart, gx, g1, gr, g2, gfull, smat, smat3,
    place_a, place_b, place_c, place_d, inv_v, inv_s, pull_s, out_a, out_b, out_d,
    w_s, q_s, x_s, r_s, p_s, ssem, rsem, id_ssem, id_rsem, lsem,
):
    me = lax.axis_index("rows")
    rep = lax.axis_index("rep")
    items = tv.shape[0]
    length, users = ids_ref.shape
    width = tv.shape[1]
    bucket = users * length // rows
    quarter = items // reps
    halves = users // width
    steps = ring_steps(rows)

    def pick(i, values):
        d = jnp.int32(values[0])
        for k in range(1, len(values)):
            d = jnp.where(i == k, values[k], d)
        return d

    def step_of(i):
        return pick(i, steps)

    meets = [steps.index(opposite(d)) for d in steps]
    stops = (0, 4, 14, rows - 9, rows - 1)
    first_late = stops[3]
    own_slot = first_late
    zero_row = (own_slot + 1) * bucket
    late_rows = (rows - 1 - first_late) * bucket

    def table_part(q):
        at = pl.multiple_of(lax.rem(rep + q, reps) * quarter, quarter)
        return pltpu.make_async_copy(table_ref.at[pl.ds(at, quarter)], tv.at[pl.ds(at, quarter)], lsem.at[q])

    small = [
        pltpu.make_async_copy(src, dst, lsem.at[reps + 2 + i])
        for i, (src, dst) in enumerate(((ids_hbm, ids_ref), (rat_hbm, rat_ref), (cnt_hbm, cnt_ref), (ub_hbm, ub_ref)))
    ]
    for copy in small:
        copy.start()
    for q in range(reps):
        table_part(q).start()

    barrier = pltpu.get_barrier_semaphore()

    def next_row(i):
        t = me + i
        return jnp.where(t >= rows, t - rows, t)

    def greet(i, c):
        pl.semaphore_signal(barrier, 1, device_id={"rows": next_row(i)}, device_id_type=MESH)
        return c

    lax.fori_loop(1, rows, greet, 0)
    near = 2 * reps
    core = me % 2
    here = core * reps + rep

    def near_peer(i):
        g = lax.rem(here + i, near)
        return g, me - core + g // reps, g % reps

    def greet_near(i, c):
        _, t, q = near_peer(i)
        pl.semaphore_signal(barrier, 1, device_id={"rows": t, "rep": q}, device_id_type=MESH)
        return c

    lax.fori_loop(1, reps, greet_near, 0)
    lax.fori_loop(reps + 1, near, greet_near, 0)

    for copy in small:
        copy.wait()

    ids = jnp.concatenate([ids_ref[:, pl.ds(h * width, width)] for h in range(halves)], axis=0)
    owner = ids // items
    local = ids % items
    local_hi = (local // 128).astype(jnp.float32)
    local_lo = (local % 128).astype(jnp.float32)
    lines = ids.shape[0]
    bucket_id = iota((rows, width), 0)
    hits = [(owner[i:i + 1] == bucket_id).astype(jnp.float32) for i in range(lines)]
    before = (iota((width, width), 0) < iota((width, width), 1)).astype(jnp.float32)
    counter = jnp.concatenate([before, jnp.ones((width, width), jnp.float32)], axis=1).astype(jnp.bfloat16)
    counted = dot(jnp.concatenate(hits, axis=0).astype(jnp.bfloat16), counter, ((1,), (0,)), None)
    seen = jnp.zeros((rows, width), jnp.float32)
    ranks = []
    for i in range(lines):
        part = counted[i * rows:(i + 1) * rows]
        ranks.append(jnp.sum(hits[i] * (part[:, :width] + seen), axis=0, keepdims=True))
        seen = seen + part[:, width:]
    rank = jnp.concatenate(ranks, axis=0).astype(jnp.int32)
    pos_v[...] = owner * bucket + rank
    values = jnp.concatenate([jnp.concatenate([hits[i] * local_hi[i:i + 1], hits[i] * local_lo[i:i + 1]], axis=0) for i in range(lines)], axis=1)
    slots = iota((bucket, width), 0)
    picks = jnp.concatenate([(rank[i:i + 1] == slots).astype(jnp.float32) for i in range(lines)], axis=1)
    compact = dot(values.astype(jnp.bfloat16), picks.astype(jnp.bfloat16), ((1,), (1,)), None)
    compact = jnp.clip((compact[:rows] * 128.0 + compact[rows:]).astype(jnp.int32), 0, items - 1)
    for b in range(rows):
        cid[b] = compact[b:b + 1]

    pl.semaphore_wait(barrier, rows - 1 + near - 2)

    def to_row(t, src, dst, which):
        return pltpu.make_async_remote_copy(
            src_ref=src, dst_ref=dst, send_sem=ssem.at[which], recv_sem=rsem.at[which],
            device_id={"rows": t}, device_id_type=MESH)

    def to_rep(q, src, dst, which):
        return pltpu.make_async_remote_copy(
            src_ref=src, dst_ref=dst, send_sem=ssem.at[which], recv_sem=rsem.at[which],
            device_id={"rep": q}, device_id_type=MESH)

    def each_row(fn):
        def go(i, c):
            fn(next_row(i))
            return c

        lax.fori_loop(1, rows, go, 0)

    def each_rep(fn):
        for q in range(1, reps):
            fn(lax.rem(rep + q, reps))

    def drain(sem, ref):
        pltpu.make_async_copy(ref, ref, sem).wait()

    turned = [lax.rem(me // 8 + dz, 4) * 8 for dz in range(4)]
    beside = [lax.rem(me // 2 + dy, 4) * 2 for dy in range(4)]
    for d in steps:
        t = turned[d // 8] + beside[d // 2 % 4] + (core if d % 2 == 0 else 1 - core)
        slot = steps.index(opposite(d))
        which = 0 if slot < stops[1] else 1
        pltpu.make_async_remote_copy(
            src_ref=cid.at[t], dst_ref=rid.at[slot], send_sem=id_ssem.at[0], recv_sem=id_rsem.at[which],
            device_id={"rows": t}, device_id_type=MESH).start()
    rid[rows - 1] = cid[me]

    share = quarter // 8

    table_part(0).wait()
    gram = jnp.zeros((width, width), jnp.float32)
    for i in range(8):
        part = tv[pl.ds(pl.multiple_of(rep * quarter + i * share, share), share), :]
        gram = gram + dot(part, part, ((0,), (0,)))
    gpart[...] = gram
    chunk = width // reps

    def chunk_of(q):
        return pl.ds(pl.multiple_of(q * chunk, chunk), chunk)

    each_rep(lambda q: to_rep(q, gpart.at[chunk_of(q)], gx.at[chunk_of(rep)], GRAM_X).start())
    gx[chunk_of(rep), :] = gpart[chunk_of(rep), :]
    for q in range(1, reps):
        table_part(q).wait()

    def fetch(i, dst, base):
        for k in range(bucket):
            dst[pl.ds(base + k, 1), :] = tv[pl.ds(rid_s[i, 0, k], 1), :]

    def take_ids(part, first, last):
        drain(id_rsem.at[part], rid.at[pl.ds(first, min(last, rows - 1) - first)])
        got = pl.ds(first, last - first)
        rid[got] = jnp.clip(rid[got], 0, items - 1)
        copy = pltpu.make_async_copy(rid.at[got], rid_s.at[got], lsem.at[reps])
        copy.start()
        copy.wait()

    def serve(late):
        def go(i, t):
            base = pl.multiple_of(t * bucket, bucket)
            fetch(i, sendb, base)
            after = shifted(me, step_of(i + 1))
            slot = pick(i, meets) - (first_late if late else 0)
            at = pl.multiple_of(slot * bucket, bucket)
            dst = lateb if late else earlyb
            to_row(t, sendb.at[pl.ds(base, bucket)], dst.at[pl.ds(at, bucket)], LATE if late else EARLY).start()
            return after

        return go

    take_ids(0, 0, stops[1])
    upcoming = shifted(me, jnp.int32(steps[0]))

    def serve_group(g, t):
        return lax.fori_loop(stops[g], stops[g + 1], serve(g == 3), t)

    upcoming = serve_group(0, upcoming)
    take_ids(1, stops[1], rows)

    drain(rsem.at[GRAM_X], gx.at[pl.ds(0, width - chunk)])
    total = gx[0:chunk, :]
    for q in range(1, reps):
        total = total + gx[q * chunk:(q + 1) * chunk, :]
    for b in range(rows):
        g1[b] = total[b:b + 1]
    each_row(lambda t: to_row(t, g1.at[t], gr.at[me], GRAM_SUM).start())
    gr[me] = g1[me]

    upcoming = serve_group(1, upcoming)

    ub = ub_ref[...]
    home = ub // users
    home_b = jnp.broadcast_to(home, (users, users))
    home_c = jnp.transpose(home_b)
    earlier = iota((users, users), 0) < iota((users, users), 1)
    twin = jnp.sum(jnp.where(earlier & (home_b == home_c), 1.0, 0.0), axis=0, keepdims=True).astype(jnp.int32)
    group = users // near
    far = rows // 2
    home_row, home_rep = home // reps, home % reps
    leave = ((home_row % 2) * reps + home_rep) * group + twin * far + home_row // 2
    hot = (iota((users, users), 0) == home * 2 + twin).astype(jnp.float32)
    hot_near = (iota((users, users), 0) == leave).astype(jnp.float32)
    place = jnp.sum(hot_near * (ub % users).astype(jnp.float32), axis=1, keepdims=True)
    place_a[...] = jnp.broadcast_to(place, (users, width))

    def group_of(g):
        return pl.ds(pl.multiple_of(g * group, group), group)

    def leave_near(a, b, which):
        def go(i, c):
            g, t, q = near_peer(i)
            pltpu.make_async_remote_copy(
                src_ref=a.at[group_of(g)], dst_ref=b.at[group_of(here)], send_sem=ssem.at[which], recv_sem=rsem.at[which],
                device_id={"rows": t, "rep": q}, device_id_type=MESH).start()
            return c

        lax.fori_loop(1, near, go, 0)
        b[group_of(here), :] = a[group_of(here), :]

    pieces = users // far
    spot = me // 2

    def piece_of(t):
        return pl.ds(pl.multiple_of(t * pieces, pieces), pieces)

    def leave_far(b, c, d, before, which):
        drain(rsem.at[before], b.at[pl.ds(0, users - group)])
        for t in range(far):
            for j in range(pieces):
                at = t * pieces + j
                c[at:at + 1, :] = b[j * far + t:j * far + t + 1, :]

        def go(i, k):
            t = lax.rem(spot + i, far)
            to_row(2 * t + core, c.at[piece_of(t)], d.at[piece_of(spot)], which).start()
            return k

        lax.fori_loop(1, far, go, 0)
        d[piece_of(spot), :] = c[piece_of(spot), :]

    def arrived(d, which):
        drain(rsem.at[which], d.at[pl.ds(0, users - pieces)])

    leave_near(place_a, place_b, PLACE_NEAR)

    live = iota((length, users), 0) < cnt_ref[...]
    entry = jnp.concatenate([pos_v[h * length:(h + 1) * length, :] for h in range(halves)], axis=1).astype(jnp.float32)
    lists = jnp.concatenate([jnp.where(live, rat_ref[...], 0.0), jnp.where(live, 1.0 + rat_ref[...], 0.0), entry], axis=0)
    lists = dot(jnp.concatenate(halve(lists), axis=0), hot.astype(jnp.bfloat16), ((1,), (1,)), None)
    lists = lists[:3 * length] + lists[3 * length:]
    w_s[...] = lists[:length]
    pull_s[...] = lists[length:2 * length]
    entry = jnp.concatenate([lists[2 * length:, h * width:(h + 1) * width] for h in range(halves)], axis=0)
    entry = jnp.clip(entry.astype(jnp.int32), 0, users * length - 1)
    holder = entry // bucket
    slot = jnp.full(holder.shape, own_slot, jnp.int32)
    for i, d in enumerate(steps):
        t = turned[d // 8] + beside[d // 2 % 4] + (core if d % 2 == 0 else 1 - core)
        slot = jnp.where(holder == t, i if i < first_late else i + 1, slot)
    entry = slot * bucket + entry % bucket
    late_v[...] = entry - zero_row
    pos_v[...] = jnp.minimum(entry, zero_row)
    pos_copy = pltpu.make_async_copy(pos_v, pos_s, lsem.at[reps + 1])
    pos_copy.start()
    earlyb[pl.ds(zero_row, 8), :] = jnp.zeros((8, width), jnp.float32)

    drain(rsem.at[GRAM_SUM], gr.at[pl.ds(0, rows - 1)])
    g2[0] = jnp.sum(gr[...], axis=0)
    each_row(lambda t: to_row(t, g2.at[0], gfull.at[rep, me], GRAM_ALL).start())
    gfull[rep, me] = g2[0]

    upcoming = serve_group(2, upcoming)

    upcoming = serve_group(3, upcoming)
    fetch(rows - 1, earlyb, own_slot * bucket)
    def mark(b, c):
        for u in range(2):
            want = late_v[pl.ds(2 * b + u, 1), :]
            late_hot[b, :, u * width:(u + 1) * width] = (iota((late_rows, width), 0) == want).astype(jnp.float32).astype(jnp.bfloat16)
        return c

    lax.fori_loop(0, lines // 2, mark, 0)
    drain(rsem.at[GRAM_ALL], gr.at[pl.ds(0, rows - 1)])
    each_rep(lambda q: to_rep(q, gfull.at[rep], gfull.at[rep], GRAM_BACK).start())
    leave_far(place_b, place_c, place_d, PLACE_NEAR, PLACE_FAR)

    pos_copy.wait()
    drain(rsem.at[EARLY], earlyb.at[pl.ds(0, first_late * bucket)])

    def gather(i, dst):
        for k in range(width):
            dst[pl.ds(k, 1), :] = earlyb[pl.ds(pos_s[i, k], 1), :]

    def turn(i, c):
        gather(2 * i + 1, blk_b)
        lt[2 * i] = jnp.transpose(blk_a[...])
        gather(jnp.minimum(2 * i + 2, lines - 1), blk_a)
        lt[2 * i + 1] = jnp.transpose(blk_b[...])
        return c

    gather(0, blk_a)
    lax.fori_loop(0, lines // 2, turn, 0)

    drain(rsem.at[GRAM_BACK], gfull.at[pl.ds(0, reps - 1)])
    scale = GRAM_WEIGHT * width / (items * rows)
    for q in range(reps):
        for b in range(rows):
            smat[q * chunk + b:q * chunk + b + 1, :] = gfull[q, b] * scale
    eye = (iota((width, width), 0) == iota((width, width), 1)).astype(jnp.float32)
    smat_hi, smat_lo = halve(smat[...] + REG_WEIGHT * eye)
    for k, piece in enumerate((smat_hi, smat_lo, smat_hi)):
        smat3[:, k * width:(k + 1) * width] = piece

    arrived(place_d, PLACE_FAR)
    place = place_d[...].astype(jnp.int32)
    came = iota((users, width), 0).astype(jnp.float32)
    for h in range(halves):
        here_is = jnp.where(place == iota((users, width), 1) + h * width, came, 0.0)
        inv_v[h:h + 1, :] = jnp.clip(jnp.sum(here_is, axis=0, keepdims=True).astype(jnp.int32), 0, users - 1)
    inv_copy = pltpu.make_async_copy(inv_v, inv_s, lsem.at[0])
    inv_copy.start()
    x_s[...] = jnp.zeros_like(x_s)
    inv_copy.wait()
    drain(rsem.at[LATE], lateb)
    for c in range(late_rows // width):
        columns = slice(c * width, (c + 1) * width)
        late_hi, late_lo = halve(jnp.transpose(lateb[columns, :]))
        late_turned[:width, columns] = late_hi
        late_turned[width:, columns] = late_lo
    for b in range(lines // 2):
        more = dot(late_turned[...], late_hot[b], ((1,), (0,)), None)
        for u in range(2):
            columns = slice(u * width, (u + 1) * width)
            lt[2 * b + u] = lt[2 * b + u] + more[:width, columns] + more[width:, columns]

    for h in range(halves):
        half = slice(h * width, (h + 1) * width)
        rhs = jnp.zeros((width, width), jnp.float32)
        for l in range(length):
            rhs = rhs + lt[h * length + l] * pull_s[l:l + 1, half]
        r_s[:, half] = rhs
        p_s[:, half] = rhs

    def iterate(i, norms):
        p_hi, p_lo = halve(p_s[...])
        q_s[...] = dot(smat3[...], jnp.concatenate([p_hi, p_hi, p_lo], axis=0), ((1,), (0,)), None)
        out = []
        for h in range(halves):
            half = slice(h * width, (h + 1) * width)
            direc = p_s[:, half]
            image = jnp.zeros((width, width), jnp.float32)
            for l in range(length):
                rows_l = lt[h * length + l]
                proj = jnp.sum(rows_l * direc, axis=0, keepdims=True)
                image = image + rows_l * (w_s[l:l + 1, half] * proj)
            image = image + q_s[:, half]
            alpha = norms[h] / jnp.sum(direc * image, axis=0, keepdims=True)
            x_s[:, half] = x_s[:, half] + alpha * direc
            resid = r_s[:, half] - alpha * image
            r_s[:, half] = resid
            norm_next = jnp.sum(resid * resid, axis=0, keepdims=True)
            p_s[:, half] = resid + norm_next / norms[h] * direc
            out.append(norm_next)
        return tuple(out)

    start = []
    for h in range(halves):
        first = r_s[:, h * width:(h + 1) * width]
        start.append(jnp.sum(first * first, axis=0, keepdims=True))
    lax.fori_loop(0, ITERS, iterate, tuple(start))

    for h in range(halves):
        out_a[h * width:(h + 1) * width, :] = jnp.transpose(x_s[:, h * width:(h + 1) * width])
    devices = rows * reps
    mine = me * reps + rep

    def pair_of(t):
        return pl.ds(2 * t, 2)

    def leave_home(i, c):
        t = mine + i
        t = jnp.where(t >= devices, t - devices, t)
        for j in range(2):
            out_b[2 * t + j] = out_a[pl.ds(2 * t + j, 1), :]
        pltpu.make_async_remote_copy(
            src_ref=out_b.at[pair_of(t)], dst_ref=out_d.at[pair_of(mine)], send_sem=ssem.at[OUT], recv_sem=rsem.at[OUT],
            device_id={"rows": t // reps, "rep": t % reps}, device_id_type=MESH).start()
        return c

    lax.fori_loop(1, devices, leave_home, 0)
    for j in range(2):
        out_d[2 * mine + j] = out_a[pl.ds(2 * mine + j, 1), :]
    drain(rsem.at[OUT], out_d.at[pl.ds(0, users - 2)])
    for h in range(halves):
        for k in range(width):
            at = h * width + k
            out_ref[at:at + 1, :] = out_d[inv_s[h, k]]
    result = pltpu.make_async_copy(out_ref, out_hbm, lsem.at[0])
    result.start()

    drain(id_ssem.at[0], cid.at[pl.ds(0, rows - 1)])
    drain(ssem.at[EARLY], sendb.at[pl.ds(0, first_late * bucket)])
    drain(ssem.at[LATE], sendb.at[pl.ds(0, late_rows)])
    drain(ssem.at[GRAM_X], gx.at[pl.ds(0, width - chunk)])
    drain(ssem.at[GRAM_SUM], gr.at[pl.ds(0, rows - 1)])
    drain(ssem.at[GRAM_ALL], gr.at[pl.ds(0, rows - 1)])
    drain(ssem.at[GRAM_BACK], gfull.at[pl.ds(0, reps - 1)])
    drain(ssem.at[PLACE_NEAR], place_b.at[pl.ds(0, users - group)])
    drain(ssem.at[PLACE_FAR], place_d.at[pl.ds(0, users - pieces)])
    drain(ssem.at[OUT], out_b.at[pl.ds(0, users - 2)])
    result.wait()


def body(rows, reps, item_table, item_ids, ratings, counts, user_batch):
    users, length = item_ids.shape
    items, width = item_table.shape
    slots = users * length
    f32, i32, bf16 = jnp.float32, jnp.int32, jnp.bfloat16
    late = 8 * (slots // rows)
    hbm = pl.BlockSpec(memory_space=pltpu.HBM)
    square = pltpu.VMEM((width, width), f32)
    wide = pltpu.VMEM((width, users), f32)
    single = pltpu.VMEM((users, 1, width), f32)
    tall = pltpu.VMEM((users, width), f32)
    return pl.pallas_call(
        functools.partial(kernel, rows, reps),
        out_shape=jax.ShapeDtypeStruct((users, width), f32),
        in_specs=[hbm] * 5,
        out_specs=hbm,
        scratch_shapes=[
            pltpu.VMEM((length, users), i32),
            pltpu.VMEM((length, users), f32),
            pltpu.VMEM((1, users), i32),
            pltpu.VMEM((1, users), i32),
            tall,
            pltpu.VMEM((items, width), f32),
            pltpu.VMEM((slots, width), f32),
            pltpu.VMEM((slots - late + 8, width), f32),
            pltpu.VMEM((late, width), f32),
            pltpu.VMEM((slots // width, width), i32),
            pltpu.VMEM((slots // width // 2, late, 2 * width), bf16),
            pltpu.VMEM((2 * width, late), bf16),
            pltpu.VMEM((slots // width, width, width), f32),
            square, square,
            pltpu.VMEM((rows, 1, width), i32),
            pltpu.VMEM((rows, 1, width), i32),
            pltpu.SMEM((rows, 1, width), i32),
            pltpu.VMEM((slots // width, width), i32),
            pltpu.SMEM((slots // width, width), i32),
            square,
            square,
            pltpu.VMEM((rows, 1, width), f32),
            pltpu.VMEM((rows, 1, width), f32),
            pltpu.VMEM((1, 1, width), f32),
            pltpu.VMEM((reps, rows, 1, width), f32),
            square,
            pltpu.VMEM((width, 3 * width), bf16),
            tall, tall, tall, tall,
            pltpu.VMEM((users // width, width), i32),
            pltpu.SMEM((users // width, width), i32),
            pltpu.VMEM((length, users), f32),
            tall, single, single,
            pltpu.VMEM((length, users), f32),
            wide, wide, wide, wide,
            pltpu.SemaphoreType.DMA((9,)),
            pltpu.SemaphoreType.DMA((9,)),
            pltpu.SemaphoreType.DMA((1,)),
            pltpu.SemaphoreType.DMA((2,)),
            pltpu.SemaphoreType.DMA((reps + 6,)),
        ],
        compiler_params=pltpu.CompilerParams(
            collective_id=0, has_side_effects=True, vmem_limit_bytes=63 << 20
        ),
    )(item_ids.T, ratings.T, counts.reshape(1, users), user_batch.reshape(1, users), item_table)


def solution(mesh):
    in_specs = (
        P("rows", None),
        P(("rows", "rep"), None),
        P(("rows", "rep"), None),
        P(("rows", "rep")),
        P(("rows", "rep")),
    )
    out_specs = P(("rows", "rep"), None)
    step = functools.partial(body, mesh.shape["rows"], mesh.shape["rep"])
    return jax.shard_map(step, mesh=mesh, in_specs=in_specs, out_specs=out_specs, check_vma=False)
```

```python
import functools

import jax
import jax.numpy as jnp
from jax import lax
from jax.experimental import pallas as pl
from jax.experimental.pallas import tpu as pltpu
from jax.sharding import PartitionSpec as P

ITERS = 8
REG_WEIGHT = 1.0
GRAM_WEIGHT = 4.0
HIGH = lax.Precision.HIGHEST
MESH = pl.DeviceIdType.MESH

EARLY, LATE, GRAM_X, PLACE_NEAR, GRAM_SUM, PLACE_FAR, GRAM_ALL, GRAM_BACK, OUT = range(9)


def ring_steps(rows):
    def hops(d):
        dy, dz = (d // 2) % 4, d // 8
        return min(dy, 4 - dy) + min(dz, 4 - dz) or 1.5

    return sorted(range(1, rows), key=lambda d: (-hops(d), d % 2))


def opposite(d):
    return (4 - d // 8) % 4 * 8 + (4 - d // 2 % 4) % 4 * 2 + d % 2


def shifted(me, d):
    c, y, z = me % 2, (me // 2) % 4, me // 8
    dc, dy, dz = d % 2, (d // 2) % 4, d // 8
    return ((z + dz) % 4 * 4 + (y + dy) % 4) * 2 + (c + dc) % 2


def dot(a, b, dims, precision=HIGH):
    return lax.dot_general(a, b, (dims, ((), ())), precision=precision, preferred_element_type=jnp.float32)


def halve(a):
    high = a.astype(jnp.bfloat16)
    return high, (a - high.astype(jnp.float32)).astype(jnp.bfloat16)


def iota(shape, axis):
    return lax.broadcasted_iota(jnp.int32, shape, axis)


def kernel(
    rows, reps, ids_hbm, rat_hbm, cnt_hbm, ub_hbm, table_ref, out_hbm,
    ids_ref, rat_ref, cnt_ref, ub_ref, out_ref, tv, sendb, earlyb, lateb, late_v, late_hot, late_turned, lt, blk_a, blk_b, cid, rid, rid_s, pos_v, pos_s,
    gpart, gx, g1, gr, g2, gfull, smat, smat3,
    place_a, place_b, place_c, place_d, inv_v, inv_s, pull_s, out_a, out_b, out_d,
    w_s, x_s, r_s, p_s, ssem, rsem, id_ssem, id_rsem, lsem,
):
    me = lax.axis_index("rows")
    rep = lax.axis_index("rep")
    items = tv.shape[0]
    length, users = ids_ref.shape
    width = tv.shape[1]
    bucket = users * length // rows
    quarter = items // reps
    halves = users // width
    steps = ring_steps(rows)

    def pick(i, values):
        d = jnp.int32(values[0])
        for k in range(1, len(values)):
            d = jnp.where(i == k, values[k], d)
        return d

    def step_of(i):
        return pick(i, steps)

    meets = [steps.index(opposite(d)) for d in steps]
    stops = (0, 4, 14, rows - 9, rows - 1)
    first_late = stops[3]
    own_slot = first_late
    zero_row = (own_slot + 1) * bucket
    late_rows = (rows - 1 - first_late) * bucket

    def table_part(q):
        at = pl.multiple_of(lax.rem(rep + q, reps) * quarter, quarter)
        return pltpu.make_async_copy(table_ref.at[pl.ds(at, quarter)], tv.at[pl.ds(at, quarter)], lsem.at[q])

    small = [
        pltpu.make_async_copy(src, dst, lsem.at[reps + 2 + i])
        for i, (src, dst) in enumerate(((ids_hbm, ids_ref), (rat_hbm, rat_ref), (cnt_hbm, cnt_ref), (ub_hbm, ub_ref)))
    ]
    for copy in small:
        copy.start()
    for q in range(reps):
        table_part(q).start()

    barrier = pltpu.get_barrier_semaphore()

    def next_row(i):
        t = me + i
        return jnp.where(t >= rows, t - rows, t)

    def greet(i, c):
        pl.semaphore_signal(barrier, 1, device_id={"rows": next_row(i)}, device_id_type=MESH)
        return c

    lax.fori_loop(1, rows, greet, 0)
    near = 2 * reps
    core = me % 2
    here = core * reps + rep

    def near_peer(i):
        g = lax.rem(here + i, near)
        return g, me - core + g // reps, g % reps

    def greet_near(i, c):
        _, t, q = near_peer(i)
        pl.semaphore_signal(barrier, 1, device_id={"rows": t, "rep": q}, device_id_type=MESH)
        return c

    lax.fori_loop(1, reps, greet_near, 0)
    lax.fori_loop(reps + 1, near, greet_near, 0)

    for copy in small:
        copy.wait()

    ids = jnp.concatenate([ids_ref[:, pl.ds(h * width, width)] for h in range(halves)], axis=0)
    owner = ids // items
    local = ids % items
    local_hi = (local // 128).astype(jnp.float32)
    local_lo = (local % 128).astype(jnp.float32)
    lines = ids.shape[0]
    bucket_id = iota((rows, width), 0)
    hits = [(owner[i:i + 1] == bucket_id).astype(jnp.float32) for i in range(lines)]
    before = (iota((width, width), 0) < iota((width, width), 1)).astype(jnp.float32)
    counter = jnp.concatenate([before, jnp.ones((width, width), jnp.float32)], axis=1).astype(jnp.bfloat16)
    counted = dot(jnp.concatenate(hits, axis=0).astype(jnp.bfloat16), counter, ((1,), (0,)), None)
    seen = jnp.zeros((rows, width), jnp.float32)
    ranks = []
    for i in range(lines):
        part = counted[i * rows:(i + 1) * rows]
        ranks.append(jnp.sum(hits[i] * (part[:, :width] + seen), axis=0, keepdims=True))
        seen = seen + part[:, width:]
    rank = jnp.concatenate(ranks, axis=0).astype(jnp.int32)
    pos_v[...] = owner * bucket + rank
    values = jnp.concatenate([jnp.concatenate([hits[i] * local_hi[i:i + 1], hits[i] * local_lo[i:i + 1]], axis=0) for i in range(lines)], axis=1)
    slots = iota((bucket, width), 0)
    picks = jnp.concatenate([(rank[i:i + 1] == slots).astype(jnp.float32) for i in range(lines)], axis=1)
    compact = dot(values.astype(jnp.bfloat16), picks.astype(jnp.bfloat16), ((1,), (1,)), None)
    compact = jnp.clip((compact[:rows] * 128.0 + compact[rows:]).astype(jnp.int32), 0, items - 1)
    for b in range(rows):
        cid[b] = compact[b:b + 1]

    pl.semaphore_wait(barrier, rows - 1 + near - 2)

    def to_row(t, src, dst, which):
        return pltpu.make_async_remote_copy(
            src_ref=src, dst_ref=dst, send_sem=ssem.at[which], recv_sem=rsem.at[which],
            device_id={"rows": t}, device_id_type=MESH)

    def to_rep(q, src, dst, which):
        return pltpu.make_async_remote_copy(
            src_ref=src, dst_ref=dst, send_sem=ssem.at[which], recv_sem=rsem.at[which],
            device_id={"rep": q}, device_id_type=MESH)

    def each_row(fn):
        def go(i, c):
            fn(next_row(i))
            return c

        lax.fori_loop(1, rows, go, 0)

    def each_rep(fn):
        for q in range(1, reps):
            fn(lax.rem(rep + q, reps))

    def drain(sem, ref):
        pltpu.make_async_copy(ref, ref, sem).wait()

    turned = [lax.rem(me // 8 + dz, 4) * 8 for dz in range(4)]
    beside = [lax.rem(me // 2 + dy, 4) * 2 for dy in range(4)]
    for d in steps:
        t = turned[d // 8] + beside[d // 2 % 4] + (core if d % 2 == 0 else 1 - core)
        slot = steps.index(opposite(d))
        which = 0 if slot < stops[1] else 1
        pltpu.make_async_remote_copy(
            src_ref=cid.at[t], dst_ref=rid.at[slot], send_sem=id_ssem.at[0], recv_sem=id_rsem.at[which],
            device_id={"rows": t}, device_id_type=MESH).start()
    rid[rows - 1] = cid[me]

    share = quarter // 8

    table_part(0).wait()
    gram = jnp.zeros((width, width), jnp.float32)
    for i in range(8):
        part = tv[pl.ds(pl.multiple_of(rep * quarter + i * share, share), share), :]
        gram = gram + dot(part, part, ((0,), (0,)))
    gpart[...] = gram
    chunk = width // reps

    def chunk_of(q):
        return pl.ds(pl.multiple_of(q * chunk, chunk), chunk)

    each_rep(lambda q: to_rep(q, gpart.at[chunk_of(q)], gx.at[chunk_of(rep)], GRAM_X).start())
    gx[chunk_of(rep), :] = gpart[chunk_of(rep), :]
    for q in range(1, reps):
        table_part(q).wait()

    def fetch(i, dst, base):
        for k in range(bucket):
            dst[pl.ds(base + k, 1), :] = tv[pl.ds(rid_s[i, 0, k], 1), :]

    def take_ids(part, first, last):
        drain(id_rsem.at[part], rid.at[pl.ds(first, min(last, rows - 1) - first)])
        got = pl.ds(first, last - first)
        rid[got] = jnp.clip(rid[got], 0, items - 1)
        copy = pltpu.make_async_copy(rid.at[got], rid_s.at[got], lsem.at[reps])
        copy.start()
        copy.wait()

    def serve(late):
        def go(i, t):
            base = pl.multiple_of(t * bucket, bucket)
            fetch(i, sendb, base)
            after = shifted(me, step_of(i + 1))
            slot = pick(i, meets) - (first_late if late else 0)
            at = pl.multiple_of(slot * bucket, bucket)
            dst = lateb if late else earlyb
            to_row(t, sendb.at[pl.ds(base, bucket)], dst.at[pl.ds(at, bucket)], LATE if late else EARLY).start()
            return after

        return go

    take_ids(0, 0, stops[1])
    upcoming = shifted(me, jnp.int32(steps[0]))

    def serve_group(g, t):
        return lax.fori_loop(stops[g], stops[g + 1], serve(g == 3), t)

    upcoming = serve_group(0, upcoming)
    take_ids(1, stops[1], rows)

    drain(rsem.at[GRAM_X], gx.at[pl.ds(0, width - chunk)])
    total = gx[0:chunk, :]
    for q in range(1, reps):
        total = total + gx[q * chunk:(q + 1) * chunk, :]
    for b in range(rows):
        g1[b] = total[b:b + 1]
    each_row(lambda t: to_row(t, g1.at[t], gr.at[me], GRAM_SUM).start())
    gr[me] = g1[me]

    upcoming = serve_group(1, upcoming)

    ub = ub_ref[...]
    home = ub // users
    home_b = jnp.broadcast_to(home, (users, users))
    home_c = jnp.transpose(home_b)
    earlier = iota((users, users), 0) < iota((users, users), 1)
    twin = jnp.sum(jnp.where(earlier & (home_b == home_c), 1.0, 0.0), axis=0, keepdims=True).astype(jnp.int32)
    group = users // near
    far = rows // 2
    home_row, home_rep = home // reps, home % reps
    leave = ((home_row % 2) * reps + home_rep) * group + twin * far + home_row // 2
    hot = (iota((users, users), 0) == home * 2 + twin).astype(jnp.float32)
    hot_near = (iota((users, users), 0) == leave).astype(jnp.float32)
    place = jnp.sum(hot_near * (ub % users).astype(jnp.float32), axis=1, keepdims=True)
    place_a[...] = jnp.broadcast_to(place, (users, width))

    def group_of(g):
        return pl.ds(pl.multiple_of(g * group, group), group)

    def leave_near(a, b, which):
        def go(i, c):
            g, t, q = near_peer(i)
            pltpu.make_async_remote_copy(
                src_ref=a.at[group_of(g)], dst_ref=b.at[group_of(here)], send_sem=ssem.at[which], recv_sem=rsem.at[which],
                device_id={"rows": t, "rep": q}, device_id_type=MESH).start()
            return c

        lax.fori_loop(1, near, go, 0)
        b[group_of(here), :] = a[group_of(here), :]

    pieces = users // far
    spot = me // 2

    def piece_of(t):
        return pl.ds(pl.multiple_of(t * pieces, pieces), pieces)

    def leave_far(b, c, d, before, which):
        drain(rsem.at[before], b.at[pl.ds(0, users - group)])
        for t in range(far):
            for j in range(pieces):
                at = t * pieces + j
                c[at:at + 1, :] = b[j * far + t:j * far + t + 1, :]

        def go(i, k):
            t = lax.rem(spot + i, far)
            to_row(2 * t + core, c.at[piece_of(t)], d.at[piece_of(spot)], which).start()
            return k

        lax.fori_loop(1, far, go, 0)
        d[piece_of(spot), :] = c[piece_of(spot), :]

    def arrived(d, which):
        drain(rsem.at[which], d.at[pl.ds(0, users - pieces)])

    leave_near(place_a, place_b, PLACE_NEAR)

    live = iota((length, users), 0) < cnt_ref[...]
    entry = jnp.concatenate([pos_v[h * length:(h + 1) * length, :] for h in range(halves)], axis=1).astype(jnp.float32)
    lists = jnp.concatenate([jnp.where(live, rat_ref[...], 0.0), jnp.where(live, 1.0 + rat_ref[...], 0.0), entry], axis=0)
    lists = dot(jnp.concatenate(halve(lists), axis=0), hot.astype(jnp.bfloat16), ((1,), (1,)), None)
    lists = lists[:3 * length] + lists[3 * length:]
    w_s[...] = lists[:length]
    pull_s[...] = lists[length:2 * length]
    entry = jnp.concatenate([lists[2 * length:, h * width:(h + 1) * width] for h in range(halves)], axis=0)
    entry = jnp.clip(entry.astype(jnp.int32), 0, users * length - 1)
    holder = entry // bucket
    slot = jnp.full(holder.shape, own_slot, jnp.int32)
    for i, d in enumerate(steps):
        t = turned[d // 8] + beside[d // 2 % 4] + (core if d % 2 == 0 else 1 - core)
        slot = jnp.where(holder == t, i if i < first_late else i + 1, slot)
    entry = slot * bucket + entry % bucket
    late_v[...] = entry - zero_row
    pos_v[...] = jnp.minimum(entry, zero_row)
    pos_copy = pltpu.make_async_copy(pos_v, pos_s, lsem.at[reps + 1])
    pos_copy.start()
    earlyb[pl.ds(zero_row, 8), :] = jnp.zeros((8, width), jnp.float32)

    drain(rsem.at[GRAM_SUM], gr.at[pl.ds(0, rows - 1)])
    g2[0] = jnp.sum(gr[...], axis=0)
    each_row(lambda t: to_row(t, g2.at[0], gfull.at[rep, me], GRAM_ALL).start())
    gfull[rep, me] = g2[0]

    upcoming = serve_group(2, upcoming)

    upcoming = serve_group(3, upcoming)
    fetch(rows - 1, earlyb, own_slot * bucket)
    def mark(b, c):
        for u in range(2):
            want = late_v[pl.ds(2 * b + u, 1), :]
            late_hot[b, :, u * width:(u + 1) * width] = (iota((late_rows, width), 0) == want).astype(jnp.float32).astype(jnp.bfloat16)
        return c

    lax.fori_loop(0, lines // 2, mark, 0)
    drain(rsem.at[GRAM_ALL], gr.at[pl.ds(0, rows - 1)])
    each_rep(lambda q: to_rep(q, gfull.at[rep], gfull.at[rep], GRAM_BACK).start())
    leave_far(place_b, place_c, place_d, PLACE_NEAR, PLACE_FAR)

    pos_copy.wait()
    drain(rsem.at[EARLY], earlyb.at[pl.ds(0, first_late * bucket)])

    def gather(i, dst):
        for k in range(width):
            dst[pl.ds(k, 1), :] = earlyb[pl.ds(pos_s[i, k], 1), :]

    def turn(i, c):
        gather(2 * i + 1, blk_b)
        lt[2 * i] = jnp.transpose(blk_a[...])
        gather(jnp.minimum(2 * i + 2, lines - 1), blk_a)
        lt[2 * i + 1] = jnp.transpose(blk_b[...])
        return c

    gather(0, blk_a)
    lax.fori_loop(0, lines // 2, turn, 0)

    drain(rsem.at[GRAM_BACK], gfull.at[pl.ds(0, reps - 1)])
    scale = GRAM_WEIGHT * width / (items * rows)
    for q in range(reps):
        for b in range(rows):
            smat[q * chunk + b:q * chunk + b + 1, :] = gfull[q, b] * scale
    eye = (iota((width, width), 0) == iota((width, width), 1)).astype(jnp.float32)
    smat_hi, smat_lo = halve(smat[...] + REG_WEIGHT * eye)
    for k, piece in enumerate((smat_hi, smat_lo, smat_hi)):
        smat3[:, k * width:(k + 1) * width] = piece

    arrived(place_d, PLACE_FAR)
    place = place_d[...].astype(jnp.int32)
    came = iota((users, width), 0).astype(jnp.float32)
    for h in range(halves):
        here_is = jnp.where(place == iota((users, width), 1) + h * width, came, 0.0)
        inv_v[h:h + 1, :] = jnp.clip(jnp.sum(here_is, axis=0, keepdims=True).astype(jnp.int32), 0, users - 1)
    inv_copy = pltpu.make_async_copy(inv_v, inv_s, lsem.at[0])
    inv_copy.start()
    x_s[...] = jnp.zeros_like(x_s)
    inv_copy.wait()
    drain(rsem.at[LATE], lateb)
    for c in range(late_rows // width):
        columns = slice(c * width, (c + 1) * width)
        late_hi, late_lo = halve(jnp.transpose(lateb[columns, :]))
        late_turned[:width, columns] = late_hi
        late_turned[width:, columns] = late_lo
    for b in range(lines // 2):
        more = dot(late_turned[...], late_hot[b], ((1,), (0,)), None)
        for u in range(2):
            columns = slice(u * width, (u + 1) * width)
            lt[2 * b + u] = lt[2 * b + u] + more[:width, columns] + more[width:, columns]

    for h in range(halves):
        half = slice(h * width, (h + 1) * width)
        rhs = jnp.zeros((width, width), jnp.float32)
        for l in range(length):
            rhs = rhs + lt[h * length + l] * pull_s[l:l + 1, half]
        r_s[:, half] = rhs
        p_s[:, half] = rhs

    norms = []
    for h in range(halves):
        first = r_s[:, h * width:(h + 1) * width]
        norms.append(jnp.sum(first * first, axis=0, keepdims=True))
    for step in range(ITERS):
        for h in range(halves):
            half = slice(h * width, (h + 1) * width)
            direc = p_s[:, half]
            p_hi, p_lo = halve(direc)
            spread = dot(smat3[...], jnp.concatenate([p_hi, p_hi, p_lo], axis=0), ((1,), (0,)), None)
            image = jnp.zeros((width, width), jnp.float32)
            for l in range(length):
                rows_l = lt[h * length + l]
                proj = jnp.sum(rows_l * direc, axis=0, keepdims=True)
                image = image + rows_l * (w_s[l:l + 1, half] * proj)
            image = image + spread
            alpha = norms[h] / jnp.sum(direc * image, axis=0, keepdims=True)
            x_s[:, half] = x_s[:, half] + alpha * direc
            if step < ITERS - 1:
                resid = r_s[:, half] - alpha * image
                r_s[:, half] = resid
                norm_next = jnp.sum(resid * resid, axis=0, keepdims=True)
                p_s[:, half] = resid + norm_next / norms[h] * direc
                norms[h] = norm_next

    for h in range(halves):
        out_a[h * width:(h + 1) * width, :] = jnp.transpose(x_s[:, h * width:(h + 1) * width])
    devices = rows * reps
    mine = me * reps + rep

    def pair_of(t):
        return pl.ds(2 * t, 2)

    def leave_home(i, c):
        t = mine + i
        t = jnp.where(t >= devices, t - devices, t)
        for j in range(2):
            out_b[2 * t + j] = out_a[pl.ds(2 * t + j, 1), :]
        pltpu.make_async_remote_copy(
            src_ref=out_b.at[pair_of(t)], dst_ref=out_d.at[pair_of(mine)], send_sem=ssem.at[OUT], recv_sem=rsem.at[OUT],
            device_id={"rows": t // reps, "rep": t % reps}, device_id_type=MESH).start()
        return c

    lax.fori_loop(1, devices, leave_home, 0)
    for j in range(2):
        out_d[2 * mine + j] = out_a[pl.ds(2 * mine + j, 1), :]
    drain(rsem.at[OUT], out_d.at[pl.ds(0, users - 2)])
    for h in range(halves):
        for k in range(width):
            at = h * width + k
            out_ref[at:at + 1, :] = out_d[inv_s[h, k]]
    result = pltpu.make_async_copy(out_ref, out_hbm, lsem.at[0])
    result.start()

    drain(id_ssem.at[0], cid.at[pl.ds(0, rows - 1)])
    drain(ssem.at[EARLY], sendb.at[pl.ds(0, first_late * bucket)])
    drain(ssem.at[LATE], sendb.at[pl.ds(0, late_rows)])
    drain(ssem.at[GRAM_X], gx.at[pl.ds(0, width - chunk)])
    drain(ssem.at[GRAM_SUM], gr.at[pl.ds(0, rows - 1)])
    drain(ssem.at[GRAM_ALL], gr.at[pl.ds(0, rows - 1)])
    drain(ssem.at[GRAM_BACK], gfull.at[pl.ds(0, reps - 1)])
    drain(ssem.at[PLACE_NEAR], place_b.at[pl.ds(0, users - group)])
    drain(ssem.at[PLACE_FAR], place_d.at[pl.ds(0, users - pieces)])
    drain(ssem.at[OUT], out_b.at[pl.ds(0, users - 2)])
    result.wait()


def body(rows, reps, item_table, item_ids, ratings, counts, user_batch):
    users, length = item_ids.shape
    items, width = item_table.shape
    slots = users * length
    f32, i32, bf16 = jnp.float32, jnp.int32, jnp.bfloat16
    late = 8 * (slots // rows)
    hbm = pl.BlockSpec(memory_space=pltpu.HBM)
    square = pltpu.VMEM((width, width), f32)
    wide = pltpu.VMEM((width, users), f32)
    single = pltpu.VMEM((users, 1, width), f32)
    tall = pltpu.VMEM((users, width), f32)
    return pl.pallas_call(
        functools.partial(kernel, rows, reps),
        out_shape=jax.ShapeDtypeStruct((users, width), f32),
        in_specs=[hbm] * 5,
        out_specs=hbm,
        scratch_shapes=[
            pltpu.VMEM((length, users), i32),
            pltpu.VMEM((length, users), f32),
            pltpu.VMEM((1, users), i32),
            pltpu.VMEM((1, users), i32),
            tall,
            pltpu.VMEM((items, width), f32),
            pltpu.VMEM((slots, width), f32),
            pltpu.VMEM((slots - late + 8, width), f32),
            pltpu.VMEM((late, width), f32),
            pltpu.VMEM((slots // width, width), i32),
            pltpu.VMEM((slots // width // 2, late, 2 * width), bf16),
            pltpu.VMEM((2 * width, late), bf16),
            pltpu.VMEM((slots // width, width, width), f32),
            square, square,
            pltpu.VMEM((rows, 1, width), i32),
            pltpu.VMEM((rows, 1, width), i32),
            pltpu.SMEM((rows, 1, width), i32),
            pltpu.VMEM((slots // width, width), i32),
            pltpu.SMEM((slots // width, width), i32),
            square,
            square,
            pltpu.VMEM((rows, 1, width), f32),
            pltpu.VMEM((rows, 1, width), f32),
            pltpu.VMEM((1, 1, width), f32),
            pltpu.VMEM((reps, rows, 1, width), f32),
            square,
            pltpu.VMEM((width, 3 * width), bf16),
            tall, tall, tall, tall,
            pltpu.VMEM((users // width, width), i32),
            pltpu.SMEM((users // width, width), i32),
            pltpu.VMEM((length, users), f32),
            tall, single, single,
            pltpu.VMEM((length, users), f32),
            wide, wide, wide,
            pltpu.SemaphoreType.DMA((9,)),
            pltpu.SemaphoreType.DMA((9,)),
            pltpu.SemaphoreType.DMA((1,)),
            pltpu.SemaphoreType.DMA((2,)),
            pltpu.SemaphoreType.DMA((reps + 6,)),
        ],
        compiler_params=pltpu.CompilerParams(
            collective_id=0, has_side_effects=True, vmem_limit_bytes=63 << 20
        ),
    )(item_ids.T, ratings.T, counts.reshape(1, users), user_batch.reshape(1, users), item_table)


def solution(mesh):
    in_specs = (
        P("rows", None),
        P(("rows", "rep"), None),
        P(("rows", "rep"), None),
        P(("rows", "rep")),
        P(("rows", "rep")),
    )
    out_specs = P(("rows", "rep"), None)
    step = functools.partial(body, mesh.shape["rows"], mesh.shape["rep"])
    return jax.shard_map(step, mesh=mesh, in_specs=in_specs, out_specs=out_specs, check_vma=False)
```

```python
import functools

import jax
import jax.numpy as jnp
from jax import lax
from jax.experimental import pallas as pl
from jax.experimental.pallas import tpu as pltpu
from jax.sharding import PartitionSpec as P

ITERS = 8
REG_WEIGHT = 1.0
GRAM_WEIGHT = 4.0
HIGH = lax.Precision.HIGHEST
MESH = pl.DeviceIdType.MESH

EARLY, LATE, GRAM_X, PLACE_NEAR, GRAM_SUM, PLACE_FAR, GRAM_ALL, GRAM_BACK, OUT = range(9)


def ring_steps(rows):
    def hops(d):
        dy, dz = (d // 2) % 4, d // 8
        return min(dy, 4 - dy) + min(dz, 4 - dz) or 1.5

    return sorted(range(1, rows), key=lambda d: (-hops(d), d % 2))


def opposite(d):
    return (4 - d // 8) % 4 * 8 + (4 - d // 2 % 4) % 4 * 2 + d % 2


def shifted(me, d):
    c, y, z = me % 2, (me // 2) % 4, me // 8
    dc, dy, dz = d % 2, (d // 2) % 4, d // 8
    return ((z + dz) % 4 * 4 + (y + dy) % 4) * 2 + (c + dc) % 2


def dot(a, b, dims, precision=HIGH):
    return lax.dot_general(a, b, (dims, ((), ())), precision=precision, preferred_element_type=jnp.float32)


def halve(a):
    high = a.astype(jnp.bfloat16)
    return high, (a - high.astype(jnp.float32)).astype(jnp.bfloat16)


def iota(shape, axis):
    return lax.broadcasted_iota(jnp.int32, shape, axis)


def kernel(
    rows, reps, ids_hbm, rat_hbm, cnt_hbm, ub_hbm, table_ref, out_hbm,
    ids_ref, rat_ref, cnt_ref, ub_ref, out_ref, tv, sendb, earlyb, lateb, late_v, late_hot, late_turned, lt, blk_a, blk_b, cid, rid, rid_s, pos_v, pos_s,
    gpart, gx, g1, gr, g2, gfull, smat, smat3,
    place_a, place_b, place_c, place_d, inv_v, inv_s, pull_s, out_a, out_b, out_d,
    w_s, x_s, r_s, p_s, ssem, rsem, id_ssem, id_rsem, lsem,
):
    me = lax.axis_index("rows")
    rep = lax.axis_index("rep")
    items = tv.shape[0]
    length, users = ids_ref.shape
    width = tv.shape[1]
    bucket = users * length // rows
    quarter = items // reps
    halves = users // width
    steps = ring_steps(rows)

    def pick(i, values):
        d = jnp.int32(values[0])
        for k in range(1, len(values)):
            d = jnp.where(i == k, values[k], d)
        return d

    def step_of(i):
        return pick(i, steps)

    meets = [steps.index(opposite(d)) for d in steps]
    stops = (0, 4, 17, rows - 9, rows - 1)
    first_late = stops[3]
    own_slot = first_late
    zero_row = (own_slot + 1) * bucket
    late_rows = (rows - 1 - first_late) * bucket

    def table_part(q):
        at = pl.multiple_of(lax.rem(rep + q, reps) * quarter, quarter)
        return pltpu.make_async_copy(table_ref.at[pl.ds(at, quarter)], tv.at[pl.ds(at, quarter)], lsem.at[q])

    small = [
        pltpu.make_async_copy(src, dst, lsem.at[reps + 2 + i])
        for i, (src, dst) in enumerate(((ids_hbm, ids_ref), (rat_hbm, rat_ref), (cnt_hbm, cnt_ref), (ub_hbm, ub_ref)))
    ]
    for copy in small:
        copy.start()
    for q in range(reps):
        table_part(q).start()

    barrier = pltpu.get_barrier_semaphore()

    def next_row(i):
        t = me + i
        return jnp.where(t >= rows, t - rows, t)

    def greet(i, c):
        pl.semaphore_signal(barrier, 1, device_id={"rows": next_row(i)}, device_id_type=MESH)
        return c

    lax.fori_loop(1, rows, greet, 0)
    near = 2 * reps
    core = me % 2
    here = core * reps + rep

    def near_peer(i):
        g = lax.rem(here + i, near)
        return g, me - core + g // reps, g % reps

    def greet_near(i, c):
        _, t, q = near_peer(i)
        pl.semaphore_signal(barrier, 1, device_id={"rows": t, "rep": q}, device_id_type=MESH)
        return c

    lax.fori_loop(1, reps, greet_near, 0)
    lax.fori_loop(reps + 1, near, greet_near, 0)

    for copy in small:
        copy.wait()

    ids = jnp.concatenate([ids_ref[:, pl.ds(h * width, width)] for h in range(halves)], axis=0)
    owner = ids // items
    local = ids % items
    local_hi = (local // 128).astype(jnp.float32)
    local_lo = (local % 128).astype(jnp.float32)
    lines = ids.shape[0]
    bucket_id = iota((rows, width), 0)
    hits = [(owner[i:i + 1] == bucket_id).astype(jnp.float32) for i in range(lines)]
    before = (iota((width, width), 0) < iota((width, width), 1)).astype(jnp.float32)
    counter = jnp.concatenate([before, jnp.ones((width, width), jnp.float32)], axis=1).astype(jnp.bfloat16)
    counted = dot(jnp.concatenate(hits, axis=0).astype(jnp.bfloat16), counter, ((1,), (0,)), None)
    seen = jnp.zeros((rows, width), jnp.float32)
    ranks = []
    for i in range(lines):
        part = counted[i * rows:(i + 1) * rows]
        ranks.append(jnp.sum(hits[i] * (part[:, :width] + seen), axis=0, keepdims=True))
        seen = seen + part[:, width:]
    rank = jnp.concatenate(ranks, axis=0).astype(jnp.int32)
    pos_v[...] = owner * bucket + rank
    values = jnp.concatenate([jnp.concatenate([hits[i] * local_hi[i:i + 1], hits[i] * local_lo[i:i + 1]], axis=0) for i in range(lines)], axis=1)
    slots = iota((bucket, width), 0)
    picks = jnp.concatenate([(rank[i:i + 1] == slots).astype(jnp.float32) for i in range(lines)], axis=1)
    compact = dot(values.astype(jnp.bfloat16), picks.astype(jnp.bfloat16), ((1,), (1,)), None)
    compact = jnp.clip((compact[:rows] * 128.0 + compact[rows:]).astype(jnp.int32), 0, items - 1)
    for b in range(rows):
        cid[b] = compact[b:b + 1]

    pl.semaphore_wait(barrier, rows - 1 + near - 2)

    def to_row(t, src, dst, which):
        return pltpu.make_async_remote_copy(
            src_ref=src, dst_ref=dst, send_sem=ssem.at[which], recv_sem=rsem.at[which],
            device_id={"rows": t}, device_id_type=MESH)

    def to_rep(q, src, dst, which):
        return pltpu.make_async_remote_copy(
            src_ref=src, dst_ref=dst, send_sem=ssem.at[which], recv_sem=rsem.at[which],
            device_id={"rep": q}, device_id_type=MESH)

    def each_row(fn):
        def go(i, c):
            fn(next_row(i))
            return c

        lax.fori_loop(1, rows, go, 0)

    def each_rep(fn):
        for q in range(1, reps):
            fn(lax.rem(rep + q, reps))

    def drain(sem, ref):
        pltpu.make_async_copy(ref, ref, sem).wait()

    turned = [lax.rem(me // 8 + dz, 4) * 8 for dz in range(4)]
    beside = [lax.rem(me // 2 + dy, 4) * 2 for dy in range(4)]
    for d in steps:
        t = turned[d // 8] + beside[d // 2 % 4] + (core if d % 2 == 0 else 1 - core)
        slot = steps.index(opposite(d))
        which = 0 if slot < stops[1] else 1
        pltpu.make_async_remote_copy(
            src_ref=cid.at[t], dst_ref=rid.at[slot], send_sem=id_ssem.at[0], recv_sem=id_rsem.at[which],
            device_id={"rows": t}, device_id_type=MESH).start()
    rid[rows - 1] = cid[me]

    share = quarter // 8

    table_part(0).wait()
    gram = jnp.zeros((width, width), jnp.float32)
    for i in range(8):
        part = tv[pl.ds(pl.multiple_of(rep * quarter + i * share, share), share), :]
        gram = gram + dot(part, part, ((0,), (0,)))
    gpart[...] = gram
    chunk = width // reps

    def chunk_of(q):
        return pl.ds(pl.multiple_of(q * chunk, chunk), chunk)

    each_rep(lambda q: to_rep(q, gpart.at[chunk_of(q)], gx.at[chunk_of(rep)], GRAM_X).start())
    gx[chunk_of(rep), :] = gpart[chunk_of(rep), :]
    for q in range(1, reps):
        table_part(q).wait()

    def fetch(i, dst, base):
        for k in range(bucket):
            dst[pl.ds(base + k, 1), :] = tv[pl.ds(rid_s[i, 0, k], 1), :]

    def take_ids(part, first, last):
        drain(id_rsem.at[part], rid.at[pl.ds(first, min(last, rows - 1) - first)])
        got = pl.ds(first, last - first)
        rid[got] = jnp.clip(rid[got], 0, items - 1)
        copy = pltpu.make_async_copy(rid.at[got], rid_s.at[got], lsem.at[reps])
        copy.start()
        copy.wait()

    def serve(late):
        def go(i, t):
            base = pl.multiple_of(t * bucket, bucket)
            fetch(i, sendb, base)
            after = shifted(me, step_of(i + 1))
            slot = pick(i, meets) - (first_late if late else 0)
            at = pl.multiple_of(slot * bucket, bucket)
            dst = lateb if late else earlyb
            to_row(t, sendb.at[pl.ds(base, bucket)], dst.at[pl.ds(at, bucket)], LATE if late else EARLY).start()
            return after

        return go

    take_ids(0, 0, stops[1])
    upcoming = shifted(me, jnp.int32(steps[0]))

    def serve_group(g, t):
        return lax.fori_loop(stops[g], stops[g + 1], serve(g == 3), t)

    upcoming = serve_group(0, upcoming)
    take_ids(1, stops[1], rows)

    drain(rsem.at[GRAM_X], gx.at[pl.ds(0, width - chunk)])
    total = gx[0:chunk, :]
    for q in range(1, reps):
        total = total + gx[q * chunk:(q + 1) * chunk, :]
    for b in range(rows):
        g1[b] = total[b:b + 1]
    each_row(lambda t: to_row(t, g1.at[t], gr.at[me], GRAM_SUM).start())
    gr[me] = g1[me]

    upcoming = serve_group(1, upcoming)

    ub = ub_ref[...]
    home = ub // users
    home_b = jnp.broadcast_to(home, (users, users))
    home_c = jnp.transpose(home_b)
    earlier = iota((users, users), 0) < iota((users, users), 1)
    twin = jnp.sum(jnp.where(earlier & (home_b == home_c), 1.0, 0.0), axis=0, keepdims=True).astype(jnp.int32)
    group = users // near
    far = rows // 2
    home_row, home_rep = home // reps, home % reps
    leave = ((home_row % 2) * reps + home_rep) * group + twin * far + home_row // 2
    hot = (iota((users, users), 0) == home * 2 + twin).astype(jnp.float32)
    hot_near = (iota((users, users), 0) == leave).astype(jnp.float32)
    place = jnp.sum(hot_near * (ub % users).astype(jnp.float32), axis=1, keepdims=True)
    place_a[...] = jnp.broadcast_to(place, (users, width))

    def group_of(g):
        return pl.ds(pl.multiple_of(g * group, group), group)

    def leave_near(a, b, which):
        def go(i, c):
            g, t, q = near_peer(i)
            pltpu.make_async_remote_copy(
                src_ref=a.at[group_of(g)], dst_ref=b.at[group_of(here)], send_sem=ssem.at[which], recv_sem=rsem.at[which],
                device_id={"rows": t, "rep": q}, device_id_type=MESH).start()
            return c

        lax.fori_loop(1, near, go, 0)
        b[group_of(here), :] = a[group_of(here), :]

    pieces = users // far
    spot = me // 2

    def piece_of(t):
        return pl.ds(pl.multiple_of(t * pieces, pieces), pieces)

    def leave_far(b, c, d, before, which):
        drain(rsem.at[before], b.at[pl.ds(0, users - group)])
        for t in range(far):
            for j in range(pieces):
                at = t * pieces + j
                c[at:at + 1, :] = b[j * far + t:j * far + t + 1, :]

        def go(i, k):
            t = lax.rem(spot + i, far)
            to_row(2 * t + core, c.at[piece_of(t)], d.at[piece_of(spot)], which).start()
            return k

        lax.fori_loop(1, far, go, 0)
        d[piece_of(spot), :] = c[piece_of(spot), :]

    def arrived(d, which):
        drain(rsem.at[which], d.at[pl.ds(0, users - pieces)])

    leave_near(place_a, place_b, PLACE_NEAR)

    live = iota((length, users), 0) < cnt_ref[...]
    entry = jnp.concatenate([pos_v[h * length:(h + 1) * length, :] for h in range(halves)], axis=1).astype(jnp.float32)
    lists = jnp.concatenate([jnp.where(live, rat_ref[...], 0.0), jnp.where(live, 1.0 + rat_ref[...], 0.0), entry], axis=0)
    lists = dot(jnp.concatenate(halve(lists), axis=0), hot.astype(jnp.bfloat16), ((1,), (1,)), None)
    lists = lists[:3 * length] + lists[3 * length:]
    w_s[...] = lists[:length]
    pull_s[...] = lists[length:2 * length]
    entry = jnp.concatenate([lists[2 * length:, h * width:(h + 1) * width] for h in range(halves)], axis=0)
    entry = jnp.clip(entry.astype(jnp.int32), 0, users * length - 1)
    holder = entry // bucket
    slot = jnp.full(holder.shape, own_slot, jnp.int32)
    for i, d in enumerate(steps):
        t = turned[d // 8] + beside[d // 2 % 4] + (core if d % 2 == 0 else 1 - core)
        slot = jnp.where(holder == t, i if i < first_late else i + 1, slot)
    entry = slot * bucket + entry % bucket
    late_v[...] = entry - zero_row
    pos_v[...] = jnp.minimum(entry, zero_row)
    pos_copy = pltpu.make_async_copy(pos_v, pos_s, lsem.at[reps + 1])
    pos_copy.start()
    earlyb[pl.ds(zero_row, 8), :] = jnp.zeros((8, width), jnp.float32)

    drain(rsem.at[GRAM_SUM], gr.at[pl.ds(0, rows - 1)])
    g2[0] = jnp.sum(gr[...], axis=0)
    each_row(lambda t: to_row(t, g2.at[0], gfull.at[rep, me], GRAM_ALL).start())
    gfull[rep, me] = g2[0]

    upcoming = serve_group(2, upcoming)

    upcoming = serve_group(3, upcoming)
    fetch(rows - 1, earlyb, own_slot * bucket)
    def mark(b, c):
        for u in range(2):
            want = late_v[pl.ds(2 * b + u, 1), :]
            late_hot[b, :, u * width:(u + 1) * width] = (iota((late_rows, width), 0) == want).astype(jnp.float32).astype(jnp.bfloat16)
        return c

    lax.fori_loop(0, lines // 2, mark, 0)
    drain(rsem.at[GRAM_ALL], gr.at[pl.ds(0, rows - 1)])
    each_rep(lambda q: to_rep(q, gfull.at[rep], gfull.at[rep], GRAM_BACK).start())
    leave_far(place_b, place_c, place_d, PLACE_NEAR, PLACE_FAR)

    pos_copy.wait()
    drain(rsem.at[EARLY], earlyb.at[pl.ds(0, first_late * bucket)])

    def gather(i, dst):
        for k in range(width):
            dst[pl.ds(k, 1), :] = earlyb[pl.ds(pos_s[i, k], 1), :]

    def turn(i, c):
        gather(2 * i + 1, blk_b)
        lt[2 * i] = jnp.transpose(blk_a[...])
        gather(jnp.minimum(2 * i + 2, lines - 1), blk_a)
        lt[2 * i + 1] = jnp.transpose(blk_b[...])
        return c

    gather(0, blk_a)
    lax.fori_loop(0, lines // 2, turn, 0)

    drain(rsem.at[GRAM_BACK], gfull.at[pl.ds(0, reps - 1)])
    scale = GRAM_WEIGHT * width / (items * rows)
    for q in range(reps):
        for b in range(rows):
            smat[q * chunk + b:q * chunk + b + 1, :] = gfull[q, b] * scale
    eye = (iota((width, width), 0) == iota((width, width), 1)).astype(jnp.float32)
    smat_hi, smat_lo = halve(smat[...] + REG_WEIGHT * eye)
    for k, piece in enumerate((smat_hi, smat_lo, smat_hi)):
        smat3[:, k * width:(k + 1) * width] = piece

    arrived(place_d, PLACE_FAR)
    place = place_d[...].astype(jnp.int32)
    came = iota((users, width), 0).astype(jnp.float32)
    for h in range(halves):
        here_is = jnp.where(place == iota((users, width), 1) + h * width, came, 0.0)
        inv_v[h:h + 1, :] = jnp.clip(jnp.sum(here_is, axis=0, keepdims=True).astype(jnp.int32), 0, users - 1)
    inv_copy = pltpu.make_async_copy(inv_v, inv_s, lsem.at[0])
    inv_copy.start()
    x_s[...] = jnp.zeros_like(x_s)
    inv_copy.wait()
    drain(rsem.at[LATE], lateb)
    for c in range(late_rows // width):
        columns = slice(c * width, (c + 1) * width)
        late_hi, late_lo = halve(jnp.transpose(lateb[columns, :]))
        late_turned[:width, columns] = late_hi
        late_turned[width:, columns] = late_lo
    for b in range(lines // 2):
        more = dot(late_turned[...], late_hot[b], ((1,), (0,)), None)
        for u in range(2):
            columns = slice(u * width, (u + 1) * width)
            lt[2 * b + u] = lt[2 * b + u] + more[:width, columns] + more[width:, columns]

    for h in range(halves):
        half = slice(h * width, (h + 1) * width)
        rhs = jnp.zeros((width, width), jnp.float32)
        for l in range(length):
            rhs = rhs + lt[h * length + l] * pull_s[l:l + 1, half]
        r_s[:, half] = rhs
        p_s[:, half] = rhs

    norms = []
    for h in range(halves):
        first = r_s[:, h * width:(h + 1) * width]
        norms.append(jnp.sum(first * first, axis=0, keepdims=True))
    for step in range(ITERS):
        for h in range(halves):
            half = slice(h * width, (h + 1) * width)
            direc = p_s[:, half]
            p_hi, p_lo = halve(direc)
            spread = dot(smat3[...], jnp.concatenate([p_hi, p_hi, p_lo], axis=0), ((1,), (0,)), None)
            image = jnp.zeros((width, width), jnp.float32)
            for l in range(length):
                rows_l = lt[h * length + l]
                proj = jnp.sum(rows_l * direc, axis=0, keepdims=True)
                image = image + rows_l * (w_s[l:l + 1, half] * proj)
            image = image + spread
            alpha = norms[h] / jnp.sum(direc * image, axis=0, keepdims=True)
            x_s[:, half] = x_s[:, half] + alpha * direc
            if step < ITERS - 1:
                resid = r_s[:, half] - alpha * image
                r_s[:, half] = resid
                norm_next = jnp.sum(resid * resid, axis=0, keepdims=True)
                p_s[:, half] = resid + norm_next / norms[h] * direc
                norms[h] = norm_next

    for h in range(halves):
        out_a[h * width:(h + 1) * width, :] = jnp.transpose(x_s[:, h * width:(h + 1) * width])
    devices = rows * reps
    mine = me * reps + rep

    def pair_of(t):
        return pl.ds(2 * t, 2)

    def leave_home(i, c):
        t = mine + i
        t = jnp.where(t >= devices, t - devices, t)
        for j in range(2):
            out_b[2 * t + j] = out_a[pl.ds(2 * t + j, 1), :]
        pltpu.make_async_remote_copy(
            src_ref=out_b.at[pair_of(t)], dst_ref=out_d.at[pair_of(mine)], send_sem=ssem.at[OUT], recv_sem=rsem.at[OUT],
            device_id={"rows": t // reps, "rep": t % reps}, device_id_type=MESH).start()
        return c

    lax.fori_loop(1, devices, leave_home, 0)
    for j in range(2):
        out_d[2 * mine + j] = out_a[pl.ds(2 * mine + j, 1), :]
    drain(rsem.at[OUT], out_d.at[pl.ds(0, users - 2)])

    def result_part(h):
        part = pl.ds(h * width, width)
        return pltpu.make_async_copy(out_ref.at[part], out_hbm.at[part], lsem.at[h])

    for h in range(halves):
        for k in range(width):
            at = h * width + k
            out_ref[at:at + 1, :] = out_d[inv_s[h, k]]
        result_part(h).start()

    drain(id_ssem.at[0], cid.at[pl.ds(0, rows - 1)])
    drain(ssem.at[EARLY], sendb.at[pl.ds(0, first_late * bucket)])
    drain(ssem.at[LATE], sendb.at[pl.ds(0, late_rows)])
    drain(ssem.at[GRAM_X], gx.at[pl.ds(0, width - chunk)])
    drain(ssem.at[GRAM_SUM], gr.at[pl.ds(0, rows - 1)])
    drain(ssem.at[GRAM_ALL], gr.at[pl.ds(0, rows - 1)])
    drain(ssem.at[GRAM_BACK], gfull.at[pl.ds(0, reps - 1)])
    drain(ssem.at[PLACE_NEAR], place_b.at[pl.ds(0, users - group)])
    drain(ssem.at[PLACE_FAR], place_d.at[pl.ds(0, users - pieces)])
    drain(ssem.at[OUT], out_b.at[pl.ds(0, users - 2)])
    for h in range(halves):
        result_part(h).wait()


def body(rows, reps, item_table, item_ids, ratings, counts, user_batch):
    users, length = item_ids.shape
    items, width = item_table.shape
    slots = users * length
    f32, i32, bf16 = jnp.float32, jnp.int32, jnp.bfloat16
    late = 8 * (slots // rows)
    hbm = pl.BlockSpec(memory_space=pltpu.HBM)
    square = pltpu.VMEM((width, width), f32)
    wide = pltpu.VMEM((width, users), f32)
    single = pltpu.VMEM((users, 1, width), f32)
    tall = pltpu.VMEM((users, width), f32)
    return pl.pallas_call(
        functools.partial(kernel, rows, reps),
        out_shape=jax.ShapeDtypeStruct((users, width), f32),
        in_specs=[hbm] * 5,
        out_specs=hbm,
        scratch_shapes=[
            pltpu.VMEM((length, users), i32),
            pltpu.VMEM((length, users), f32),
            pltpu.VMEM((1, users), i32),
            pltpu.VMEM((1, users), i32),
            tall,
            pltpu.VMEM((items, width), f32),
            pltpu.VMEM((slots, width), f32),
            pltpu.VMEM((slots - late + 8, width), f32),
            pltpu.VMEM((late, width), f32),
            pltpu.VMEM((slots // width, width), i32),
            pltpu.VMEM((slots // width // 2, late, 2 * width), bf16),
            pltpu.VMEM((2 * width, late), bf16),
            pltpu.VMEM((slots // width, width, width), f32),
            square, square,
            pltpu.VMEM((rows, 1, width), i32),
            pltpu.VMEM((rows, 1, width), i32),
            pltpu.SMEM((rows, 1, width), i32),
            pltpu.VMEM((slots // width, width), i32),
            pltpu.SMEM((slots // width, width), i32),
            square,
            square,
            pltpu.VMEM((rows, 1, width), f32),
            pltpu.VMEM((rows, 1, width), f32),
            pltpu.VMEM((1, 1, width), f32),
            pltpu.VMEM((reps, rows, 1, width), f32),
            square,
            pltpu.VMEM((width, 3 * width), bf16),
            tall, tall, tall, tall,
            pltpu.VMEM((users // width, width), i32),
            pltpu.SMEM((users // width, width), i32),
            pltpu.VMEM((length, users), f32),
            tall, single, single,
            pltpu.VMEM((length, users), f32),
            wide, wide, wide,
            pltpu.SemaphoreType.DMA((9,)),
            pltpu.SemaphoreType.DMA((9,)),
            pltpu.SemaphoreType.DMA((1,)),
            pltpu.SemaphoreType.DMA((2,)),
            pltpu.SemaphoreType.DMA((reps + 6,)),
        ],
        compiler_params=pltpu.CompilerParams(
            collective_id=0, has_side_effects=True, vmem_limit_bytes=63 << 20
        ),
    )(item_ids.T, ratings.T, counts.reshape(1, users), user_batch.reshape(1, users), item_table)


def solution(mesh):
    in_specs = (
        P("rows", None),
        P(("rows", "rep"), None),
        P(("rows", "rep"), None),
        P(("rows", "rep")),
        P(("rows", "rep")),
    )
    out_specs = P(("rows", "rep"), None)
    step = functools.partial(body, mesh.shape["rows"], mesh.shape["rep"])
    return jax.shard_map(step, mesh=mesh, in_specs=in_specs, out_specs=out_specs, check_vma=False)
```
